256 devices in a mesh: lmaj: 16 (over z_lo, x, core), lmin: 16 (over z_hi, y).
Axes of the slice: x: 4, y: 4, z: 8 (z_hi: 4, z_lo: 2; z = z_hi * 2 + z_lo), core: 2. Of those that a mesh axis runs over, the one named last changes fastest.
Arguments:
- resid_rows: bfloat16 [512, 3584], P('lmin'), may hold values from -6 to 6
- w_encode: bfloat16 [3584, 98304], P(None, ('lmaj', 'lmin')), may hold values from -0.09375 to 0.09375
- b_encode: float32 [98304], P(('lmaj', 'lmin')), may hold values from -3 to 3
- w_decode: bfloat16 [98304, 3584], P(('lmaj', 'lmin')), may hold values from -0.01953125 to 0.01953125
- b_decode: float32 [3584], replicated, may hold values from -3 to 3
Outputs:
- grad_encode: bfloat16 [3584, 98304], P(None, ('lmaj', 'lmin'))
- grad_b_encode: float32 [98304], P(('lmaj', 'lmin'))
- grad_decode: bfloat16 [98304, 3584], P(('lmaj', 'lmin'))
- grad_b_decode: float32 [3584], replicated
The draws below stay inside these ranges and needn't reach their ends.
All inputs are finite; a program needn't handle non-finite values.
Results may differ from the reference program's by a relative error of at most 0.006.
Values may be sent and summed in bfloat16 or wider, within the bound.
No kernel may reach another device: no remote copies, remote signals or barrier semaphores. Data moves between devices by JAX's collectives and lax.ppermute only.
A program may use at most 128 MiB of HBM per device.

```python
import math
import jax
import jax.numpy as jnp
from jax import lax

D = 3584
LATENTS = 98304
ROWS = 512


def shard_levels(key, shape, pieces, least, high):
    level = 1.0
    for axis_at, shards_of in pieces:
        steps = jax.random.uniform(jax.random.fold_in(jax.random.fold_in(key, 6), axis_at), (shards_of,), jnp.float32, least / len(pieces), high / len(pieces))
        level = level * jnp.repeat(jnp.exp(steps), shape[axis_at] // shards_of).reshape((-1,) + (1,) * (len(shape) - 1 - axis_at))
    return level


def centred(key, shape, deviation, most, shards=(), kind=jnp.bfloat16):
    drawn = jax.random.normal(key, shape, jnp.float32) * deviation
    if len(shards) > 0:
        drawn = shard_levels(key, shape, shards, -0.22, 0.18) * drawn
    return jnp.clip(drawn, min=-most, max=most).astype(kind)


def setup_inputs(seed: int = 0) -> dict:
    seeds = jax.random.split(jax.random.key(seed), 6)
    resid_rows = centred(seeds[0], (ROWS, D), 1.0, 6.0, ((0, 16),))
    w_encode = centred(seeds[1], (D, LATENTS), D ** -0.5, 0.09375, ((1, 256),))
    b_encode = centred(seeds[2], (LATENTS,), 0.5, 3.0, ((0, 256),), jnp.float32)
    w_decode = centred(seeds[3], (LATENTS, D), LATENTS ** -0.5, 0.01953125, ((0, 256),))
    b_decode = centred(seeds[4], (D,), 0.5, 3.0, (), jnp.float32)
    return {"resid_rows": resid_rows, "w_encode": w_encode, "b_encode": b_encode, "w_decode": w_decode, "b_decode": b_decode}


def reference(resid_rows, w_encode, b_encode, w_decode, b_decode):
    centered = (resid_rows.astype(jnp.float32) - b_decode).astype(jnp.bfloat16)
    pre = jnp.dot(centered, w_encode, preferred_element_type=jnp.float32) + b_encode
    active = jnp.maximum(pre, 0.0)
    codes = (active * active).astype(jnp.bfloat16)
    summed = jnp.dot(codes, w_decode, preferred_element_type=jnp.float32)
    error = (summed - centered.astype(jnp.float32)).astype(jnp.bfloat16)
    factor = 1.0 / math.sqrt(ROWS)
    dec_float = w_decode.astype(jnp.float32)
    norms = jnp.sqrt(lax.optimization_barrier(jnp.sum(dec_float * dec_float, axis=1)) + 1e-06)
    code_sum = lax.optimization_barrier(jnp.sum(codes.astype(jnp.float32), axis=0))
    grad_decode = (2.0 * factor * jnp.dot(codes.T, error, preferred_element_type=jnp.float32) + 0.5 * factor * (code_sum / norms)[:, None] * dec_float).astype(jnp.bfloat16)
    back = 2.0 * factor * jnp.dot(error, w_decode.T, preferred_element_type=jnp.float32) + 0.5 * factor * norms
    dpre = back * 2.0 * active
    dpre_round = dpre.astype(jnp.bfloat16)
    grad_encode = jnp.dot(centered.T, dpre_round, preferred_element_type=jnp.float32).astype(jnp.bfloat16)
    grad_b_encode = lax.optimization_barrier(jnp.sum(dpre, axis=0))
    through = jnp.dot(w_encode.astype(jnp.float32), grad_b_encode, precision=lax.Precision.HIGHEST)
    grad_b_decode = 2.0 * factor * lax.optimization_barrier(jnp.sum(error.astype(jnp.float32), axis=0)) - through
    return (grad_encode, grad_b_encode, grad_decode, grad_b_decode)
```

```python
import math

import jax
import jax.numpy as jnp
from jax import lax
from jax.sharding import Mesh, PartitionSpec as P

LMAJ = ("zl", "x", "c")
LMIN = ("zh", "y")
Z = ("zl", "zh")
XY = ("x", "y")


def spread(block, axes, n):
    return lax.all_to_all(
        jnp.broadcast_to(block[None], (n,) + block.shape), axes, 0, 0, tiled=True
    )


def swap(block):
    return lax.ppermute(block, "c", [(0, 1), (1, 0)])


def per_device(resid_rows, w_encode, b_encode, w_decode, b_decode):
    f32, bf16 = jnp.float32, jnp.bfloat16
    local_rows, width = resid_rows.shape
    nz, nxy, nx, nzh = 8, 16, 4, 4
    total_rows = local_rows * 16
    half = total_rows // 2
    factor = 1.0 / math.sqrt(total_rows)
    core = lax.axis_index("c")
    piece = local_rows // (2 * nx)
    mine = lax.dynamic_slice_in_dim(
        resid_rows, (core * nx + lax.axis_index("x")) * piece, piece, 0
    )
    mine = (mine.astype(f32) - b_decode).astype(bf16)
    block = spread(mine, ("zh",), nzh).reshape(piece * nzh, width)
    own = spread(block, XY, nxy).reshape(half, width)
    other = swap(own)

    def encode(rows):
        pre = jnp.dot(rows, w_encode, preferred_element_type=f32) + b_encode
        active = jnp.maximum(pre, 0.0)
        return active, (active * active).astype(bf16)

    active_own, codes_own = encode(own)
    active_other, codes_other = encode(other)
    to_other = jnp.dot(codes_other, w_decode, preferred_element_type=f32).astype(bf16)
    from_other = swap(to_other)
    part = jnp.dot(codes_own, w_decode, preferred_element_type=f32) + from_other.astype(f32)
    part = part.astype(bf16).reshape(nxy, half // nxy, width)
    part = lax.all_to_all(part, XY, 0, 0, tiled=True)
    part = jnp.sum(part.astype(f32), axis=0).astype(bf16)
    few = half // nxy // nz
    part = lax.all_to_all(part.reshape(nz, few, width), Z, 0, 0, tiled=True)
    summed = jnp.sum(part.astype(f32), axis=0)
    at = (lax.axis_index("zl") * nzh + lax.axis_index("zh")) * few
    few_rows = lax.dynamic_slice_in_dim(block, at, few, 0)
    error_part = (summed - few_rows.astype(f32)).astype(bf16)
    error_block = spread(error_part, Z, nz).reshape(half // nxy, width)
    error_own = spread(error_block, XY, nxy).reshape(half, width)
    error_other = swap(error_own)

    dec_float = w_decode.astype(f32)
    norms = jnp.sqrt(jnp.sum(dec_float * dec_float, axis=1) + 1e-06)

    def backward(error, active):
        back = (
            2.0 * factor * jnp.dot(error, w_decode.T, preferred_element_type=f32)
            + 0.5 * factor * norms
        )
        return back * 2.0 * active

    dpre_own = backward(error_own, active_own)
    dpre_other = backward(error_other, active_other)
    grad_b_encode = jnp.sum(dpre_own, axis=0) + jnp.sum(dpre_other, axis=0)
    through = jnp.dot(w_encode.astype(f32), grad_b_encode, precision=lax.Precision.HIGHEST)
    through = through.reshape(width // 128, 128)
    through = through + swap(through)
    through = jnp.sum(spread(through, Z, nz), axis=0)
    through = jnp.sum(spread(through, XY, nxy), axis=0).reshape(width)

    centered = jnp.concatenate([own, other], axis=0)
    error = jnp.concatenate([error_own, error_other], axis=0)
    codes = jnp.concatenate([codes_own, codes_other], axis=0)
    dpre_round = jnp.concatenate([dpre_own, dpre_other], axis=0).astype(bf16)
    code_sum = jnp.sum(codes.astype(f32), axis=0)
    grad_decode = (
        2.0 * factor * jnp.dot(codes.T, error, preferred_element_type=f32)
        + 0.5 * factor * (code_sum / norms)[:, None] * dec_float
    ).astype(bf16)
    grad_encode = jnp.dot(centered.T, dpre_round, preferred_element_type=f32).astype(bf16)
    grad_b_decode = 2.0 * factor * jnp.sum(error.astype(f32), axis=0) - through
    return (grad_encode, grad_b_encode, grad_decode, grad_b_decode)


def solution(mesh):
    fine = Mesh(mesh.devices.reshape(2, 4, 2, 4, 4), ("zl", "x", "c", "zh", "y"))
    latents = LMAJ + LMIN
    in_specs = (P(LMIN, None), P(None, latents), P(latents), P(latents, None), P())
    out_specs = (P(None, latents), P(latents), P(latents, None), P())
    return jax.shard_map(
        per_device, mesh=fine, in_specs=in_specs, out_specs=out_specs, check_vma=False
    )
```

```python
import math

import jax
import jax.numpy as jnp
from jax import lax
from jax.sharding import Mesh, PartitionSpec as P

LMAJ = ("zl", "x", "c")
LMIN = ("zh", "y")
WIDE = ("zl", "x", "y")
NWIDE, NZH, NC = 32, 4, 2


def spread(block, axes, n):
    return lax.all_to_all(
        jnp.broadcast_to(block[None], (n,) + block.shape), axes, 0, 0, tiled=True
    )


def swap(block):
    return lax.ppermute(block, "c", [(0, 1), (1, 0)])


def per_device(resid_rows, w_encode, b_encode, w_decode, b_decode):
    f32, bf16 = jnp.float32, jnp.bfloat16
    local_rows, width = resid_rows.shape
    total_rows = local_rows * 16
    half = total_rows // NC
    rows = half // NWIDE
    factor = 1.0 / math.sqrt(total_rows)

    enc = (w_encode, swap(w_encode))
    dec = (w_decode, swap(w_decode))
    bias = (b_encode, swap(b_encode))

    piece = rows // NZH
    at = (lax.axis_index("c") * 2 + lax.axis_index("zl")) * 4 + lax.axis_index("x")
    mine = lax.dynamic_slice_in_dim(resid_rows, at * piece, piece, 0)
    mine = (mine.astype(f32) - b_decode).astype(bf16)
    block = spread(mine, ("zh",), NZH).reshape(rows, width)
    centered = spread(block, WIDE, NWIDE).reshape(half, width)

    active, codes = [], []
    for w, b in zip(enc, bias):
        a = jnp.maximum(jnp.dot(centered, w, preferred_element_type=f32) + b, 0.0)
        active.append(a)
        codes.append((a * a).astype(bf16))
    part = jnp.dot(codes[0], dec[0], preferred_element_type=f32) + jnp.dot(
        codes[1], dec[1], preferred_element_type=f32
    )
    part = part.astype(bf16).reshape(NWIDE, rows, width)
    part = lax.all_to_all(part, WIDE, 0, 0, tiled=True)
    part = jnp.sum(part.astype(f32), axis=0).astype(bf16)
    summed = jnp.sum(spread(part, ("zh",), NZH).astype(f32), axis=0)
    error_block = (summed - block.astype(f32)).astype(bf16)
    error = spread(error_block, WIDE, NWIDE).reshape(half, width)

    dec_float = [w.astype(f32) for w in dec]
    norms = [jnp.sqrt(jnp.sum(w * w, axis=1) + 1e-06) for w in dec_float]
    dpre = []
    for w, n, a in zip(dec, norms, active):
        back = 2.0 * factor * jnp.dot(error, w.T, preferred_element_type=f32) + 0.5 * factor * n
        dpre.append(back * 2.0 * a)
    bias_grad = [jnp.sum(d, axis=0) for d in dpre]

    through = -2.0 * factor / NZH * jnp.sum(error_block.astype(f32), axis=0)
    for w, g in zip(enc, bias_grad):
        through = through + jnp.dot(w.astype(f32), g, precision=lax.Precision.HIGHEST)
    through = through.reshape(width // 128, 128)
    through = through + swap(through)
    codes[1], dpre[1], through = lax.optimization_barrier((codes[1], dpre[1], through))
    through = jnp.sum(spread(through, ("zh",), NZH), axis=0)
    codes[0], dpre[0], through = lax.optimization_barrier((codes[0], dpre[0], through))
    through = jnp.sum(spread(through, WIDE, NWIDE), axis=0).reshape(width)

    def decode_part(k):
        code_sum = jnp.sum(codes[k].astype(f32), axis=0)
        return (
            2.0 * factor * jnp.dot(codes[k].T, error, preferred_element_type=f32)
            + 0.5 * factor * (code_sum / norms[k])[:, None] * dec_float[k]
        )

    def encode_part(k):
        return jnp.dot(centered.T, dpre[k].astype(bf16), preferred_element_type=f32)

    from_decode = swap(decode_part(1).astype(bf16))
    from_encode = swap(encode_part(1).astype(bf16))
    grad_decode = (decode_part(0) + from_decode.astype(f32)).astype(bf16)
    grad_encode = (encode_part(0) + from_encode.astype(f32)).astype(bf16)
    grad_b_encode = bias_grad[0] + swap(bias_grad[1])
    return (grad_encode, grad_b_encode, grad_decode, -through)


def solution(mesh):
    fine = Mesh(mesh.devices.reshape(2, 4, 2, 4, 4), ("zl", "x", "c", "zh", "y"))
    latents = LMAJ + LMIN
    in_specs = (P(LMIN, None), P(None, latents), P(latents), P(latents, None), P())
    out_specs = (P(None, latents), P(latents), P(latents, None), P())
    return jax.shard_map(
        per_device, mesh=fine, in_specs=in_specs, out_specs=out_specs, check_vma=False
    )
```

```python
import functools
import math

import jax
import jax.numpy as jnp
from jax import lax
from jax.experimental import pallas as pl
from jax.experimental.pallas import tpu as pltpu
from jax.sharding import Mesh, PartitionSpec as P

LMAJ = ("zl", "x", "c")
LMIN = ("zh", "y")
WIDE = ("zl", "x", "y")
NWIDE, NZH, NC = 32, 4, 2
CHUNK = 512
VMEM_BYTES = 61 * 1024 * 1024
ANY = pl.BlockSpec(memory_space=pl.ANY)
VMEM = pl.BlockSpec(memory_space=pltpu.VMEM)
f32, bf16 = jnp.float32, jnp.bfloat16


def spread(block, axes, n):
    return lax.all_to_all(
        jnp.broadcast_to(block[None], (n,) + block.shape), axes, 0, 0, tiled=True
    )


def swap(block):
    return lax.ppermute(block, "c", [(0, 1), (1, 0)])


def forward_kernel(
    rows_hbm, enc0, enc1, dec0, dec1, bias0, bias1,
    active0, active1, codes0, codes1, part_hbm,
    rows, enc, dec, pre, codes, part, sem_in, sem_enc, sem_dec, sem_out,
):
    width, latents = enc.shape
    mine = latents // 2
    steps = width // CHUNK

    def at(k):
        return pl.ds(pl.multiple_of(k * CHUNK, CHUNK), CHUNK)

    def enc_copies(k):
        return (
            pltpu.make_async_copy(rows_hbm.at[:, at(k)], rows.at[:, at(k)], sem_in.at[k]),
            pltpu.make_async_copy(enc0.at[at(k)], enc.at[at(k), :mine], sem_enc.at[0, k]),
            pltpu.make_async_copy(enc1.at[at(k)], enc.at[at(k), mine:], sem_enc.at[1, k]),
        )

    def dec_copies(k):
        return (
            pltpu.make_async_copy(dec0.at[:, at(k)], dec.at[:mine, at(k)], sem_dec.at[0, k]),
            pltpu.make_async_copy(dec1.at[:, at(k)], dec.at[mine:, at(k)], sem_dec.at[1, k]),
        )

    for copies in (enc_copies, dec_copies):
        for k in range(steps):
            for copy in copies(k):
                copy.start()

    pre[:, :mine] = jnp.broadcast_to(bias0[...], (pre.shape[0], mine))
    pre[:, mine:] = jnp.broadcast_to(bias1[...], (pre.shape[0], mine))

    @pl.loop(0, steps)
    def _(k):
        for copy in enc_copies(k):
            copy.wait()
        pre[...] += jnp.dot(rows[:, at(k)], enc[at(k), :], preferred_element_type=f32)

    active = jnp.maximum(pre[...], 0.0)
    active0[...] = active[:, :mine]
    active1[...] = active[:, mine:]
    codes[...] = (active * active).astype(bf16)
    codes0[...] = codes[:, :mine]
    codes1[...] = codes[:, mine:]

    def out_copy(k):
        return pltpu.make_async_copy(part.at[:, at(k)], part_hbm.at[:, at(k)], sem_out.at[k])

    @pl.loop(0, steps)
    def _(k):
        for copy in dec_copies(k):
            copy.wait()
        part[:, at(k)] = jnp.dot(
            codes[...], dec[:, at(k)], preferred_element_type=f32
        ).astype(bf16)
        out_copy(k).start()

    for k in range(steps):
        out_copy(k).wait()


def forward(rows, enc, bias, dec):
    count, width = rows.shape
    mine = enc[0].shape[1]
    steps = width // CHUNK
    flat = jax.ShapeDtypeStruct((count, mine), f32)
    half = jax.ShapeDtypeStruct((count, mine), bf16)
    return pl.pallas_call(
        forward_kernel,
        out_shape=(flat, flat, half, half, jax.ShapeDtypeStruct((count, width), bf16)),
        in_specs=[ANY] * 5 + [VMEM] * 2,
        out_specs=(VMEM,) * 4 + (ANY,),
        scratch_shapes=[
            pltpu.VMEM((count, width), bf16),
            pltpu.VMEM((width, 2 * mine), bf16),
            pltpu.VMEM((2 * mine, width), bf16),
            pltpu.VMEM((count, 2 * mine), f32),
            pltpu.VMEM((count, 2 * mine), bf16),
            pltpu.VMEM((count, width), bf16),
            pltpu.SemaphoreType.DMA((steps,)),
            pltpu.SemaphoreType.DMA((2, steps)),
            pltpu.SemaphoreType.DMA((2, steps)),
            pltpu.SemaphoreType.DMA((steps,)),
        ],
        compiler_params=pltpu.CompilerParams(vmem_limit_bytes=VMEM_BYTES),
        cost_estimate=pl.CostEstimate(
            flops=8 * count * width * mine, bytes_accessed=13_000_000, transcendentals=0
        ),
        name="forward",
    )(rows, *enc, *dec, *(b.reshape(1, mine) for b in bias))


def backward_kernel(
    factor, error_hbm, dec0, dec1, enc0, enc1, active0, active1, norms0, norms1,
    dpre0, dpre1, sums, through,
    error, dec, enc, back, sem_in, sem_enc, sem_dec,
):
    width, latents = enc.shape
    mine = latents // 2
    steps = width // CHUNK

    def at(k):
        return pl.ds(pl.multiple_of(k * CHUNK, CHUNK), CHUNK)

    def dec_copies(k):
        return (
            pltpu.make_async_copy(error_hbm.at[:, at(k)], error.at[:, at(k)], sem_in.at[k]),
            pltpu.make_async_copy(dec0.at[:, at(k)], dec.at[:mine, at(k)], sem_dec.at[0, k]),
            pltpu.make_async_copy(dec1.at[:, at(k)], dec.at[mine:, at(k)], sem_dec.at[1, k]),
        )

    def enc_copies(k):
        return (
            pltpu.make_async_copy(enc0.at[at(k)], enc.at[at(k), :mine], sem_enc.at[0, k]),
            pltpu.make_async_copy(enc1.at[at(k)], enc.at[at(k), mine:], sem_enc.at[1, k]),
        )

    for copies in (dec_copies, enc_copies):
        for k in range(steps):
            for copy in copies(k):
                copy.start()

    back[...] = jnp.zeros_like(back)

    @pl.loop(0, steps)
    def _(k):
        for copy in dec_copies(k):
            copy.wait()
        back[...] += lax.dot_general(
            error[:, at(k)], dec[:, at(k)], (((1,), (1,)), ((), ())),
            preferred_element_type=f32,
        )

    def finish(columns, norms, active, dpre):
        value = (2.0 * factor * back[:, columns] + 0.5 * factor * norms[...]) * 2.0 * active[...]
        dpre[...] = value.astype(bf16)
        return jnp.sum(value, axis=0, keepdims=True)

    total = jnp.concatenate(
        [
            finish(slice(0, mine), norms0, active0, dpre0),
            finish(slice(mine, latents), norms1, active1, dpre1),
        ],
        axis=1,
    )
    sums[...] = total
    first = total.astype(bf16)
    rest = total - first.astype(f32)
    second = rest.astype(bf16)
    third = (rest - second.astype(f32)).astype(bf16)
    parts = jnp.concatenate(
        [first, second, third, jnp.zeros((13, latents), bf16)], axis=0
    )

    @pl.loop(0, steps)
    def _(k):
        for copy in enc_copies(k):
            copy.wait()
        product = lax.dot_general(
            parts, enc[at(k), :], (((1,), (1,)), ((), ())), preferred_element_type=f32
        )
        through[:, at(k)] = product[0:1] + product[1:2] + product[2:3]


def backward(error, dec, enc, active, norms, factor):
    count, width = error.shape
    mine = enc[0].shape[1]
    steps = width // CHUNK
    half = jax.ShapeDtypeStruct((count, mine), bf16)
    return pl.pallas_call(
        functools.partial(backward_kernel, factor),
        out_shape=(
            half,
            half,
            jax.ShapeDtypeStruct((1, 2 * mine), f32),
            jax.ShapeDtypeStruct((1, width), f32),
        ),
        in_specs=[ANY] * 5 + [VMEM] * 4,
        out_specs=(VMEM,) * 4,
        scratch_shapes=[
            pltpu.VMEM((count, width), bf16),
            pltpu.VMEM((2 * mine, width), bf16),
            pltpu.VMEM((width, 2 * mine), bf16),
            pltpu.VMEM((count, 2 * mine), f32),
            pltpu.SemaphoreType.DMA((steps,)),
            pltpu.SemaphoreType.DMA((2, steps)),
            pltpu.SemaphoreType.DMA((2, steps)),
        ],
        compiler_params=pltpu.CompilerParams(vmem_limit_bytes=VMEM_BYTES),
        cost_estimate=pl.CostEstimate(
            flops=6 * count * width * mine, bytes_accessed=13_000_000, transcendentals=0
        ),
        name="backward",
    )(error, *dec, *enc, *active, *(n.reshape(1, mine) for n in norms))


def per_device(resid_rows, w_encode, b_encode, w_decode, b_decode):
    local_rows, width = resid_rows.shape
    total_rows = local_rows * 16
    half = total_rows // NC
    rows = half // NWIDE
    factor = 1.0 / math.sqrt(total_rows)

    enc = (w_encode, swap(w_encode))
    dec = (w_decode, swap(w_decode))
    bias = (b_encode, swap(b_encode))

    piece = rows // NZH
    at = (lax.axis_index("c") * 2 + lax.axis_index("zl")) * 4 + lax.axis_index("x")
    mine = lax.dynamic_slice_in_dim(resid_rows, at * piece, piece, 0)
    mine = (mine.astype(f32) - b_decode).astype(bf16)
    block = spread(mine, ("zh",), NZH).reshape(rows, width)
    centered = spread(block, WIDE, NWIDE).reshape(half, width)
    dec_float = w_decode.astype(f32)
    norms = jnp.sqrt(jnp.sum(dec_float * dec_float, axis=1) + 1e-06)
    centered, norms, their_norms = lax.optimization_barrier((centered, norms, swap(norms)))

    active0, active1, codes0, codes1, part = forward(centered, enc, bias, dec)
    part = lax.all_to_all(part.reshape(NWIDE, rows, width), WIDE, 0, 0, tiled=True)
    all_codes = jnp.concatenate([codes0, swap(codes1)], axis=0)
    code_sum = jnp.sum(all_codes.astype(f32), axis=0)
    part, all_codes, code_sum, their_rows = lax.optimization_barrier(
        (part, all_codes, code_sum, swap(centered))
    )
    part = jnp.sum(part.astype(f32), axis=0).astype(bf16)
    summed = jnp.sum(spread(part, ("zh",), NZH).astype(f32), axis=0)
    error_block = (summed - block.astype(f32)).astype(bf16)
    error = spread(error_block, WIDE, NWIDE).reshape(half, width)
    block_sum = 2.0 * factor / NZH * jnp.sum(error_block.astype(f32), axis=0)
    error, block_sum = lax.optimization_barrier((error, block_sum))
    dpre0, dpre1, sums, through = backward(
        error, dec, enc, (active0, active1), (norms, their_norms), factor
    )

    mine = w_encode.shape[1]
    all_dpre = jnp.concatenate([dpre0, swap(dpre1)], axis=0)
    all_rows = jnp.concatenate([centered, their_rows], axis=0)
    all_error = jnp.concatenate([error, swap(error)], axis=0)

    through = (through.reshape(width) - block_sum).reshape(width // 128, 128)
    through = through + swap(through)
    through, all_codes = lax.optimization_barrier((through, all_codes))
    through = spread(through, ("zh",), NZH)
    grad_decode = (
        2.0 * factor * jnp.dot(all_codes.T, all_error, preferred_element_type=f32)
        + 0.5 * factor * (code_sum / norms)[:, None] * dec_float
    ).astype(bf16)
    through, grad_decode, all_dpre = lax.optimization_barrier((through, grad_decode, all_dpre))
    through = jnp.sum(spread(jnp.sum(through, axis=0), WIDE, NWIDE), axis=0).reshape(width)
    grad_encode = jnp.dot(all_rows.T, all_dpre, preferred_element_type=f32).astype(bf16)
    grad_b_encode = sums[0, :mine] + swap(sums[0, mine:])
    return (grad_encode, grad_b_encode, grad_decode, -through)


def solution(mesh):
    fine = Mesh(mesh.devices.reshape(2, 4, 2, 4, 4), ("zl", "x", "c", "zh", "y"))
    latents = LMAJ + LMIN
    in_specs = (P(LMIN, None), P(None, latents), P(latents), P(latents, None), P())
    out_specs = (P(None, latents), P(latents), P(latents, None), P())
    return jax.shard_map(
        per_device, mesh=fine, in_specs=in_specs, out_specs=out_specs, check_vma=False
    )
```

```python
import math

import jax
import jax.numpy as jnp
from jax import lax
from jax.sharding import Mesh, PartitionSpec as P

LMAJ = ("zl", "x", "c")
LMIN = ("zh", "y")
WIDE, NWIDE = ("zl", "x", "y"), 32
XY, NXY = ("x", "y"), 16
Z, NZ = ("zl", "zh"), 8
ZH, NZH = ("zh",), 4
f32, bf16 = jnp.float32, jnp.bfloat16


def spread(block, axes, n):
    return lax.all_to_all(
        jnp.broadcast_to(block[None], (n,) + block.shape), axes, 0, 0, tiled=True
    )


def swap(block):
    return lax.ppermute(block, "c", [(0, 1), (1, 0)])


def tie(*values):
    return lax.optimization_barrier(values)


def per_device(resid_rows, w_encode, b_encode, w_decode, b_decode):
    local_rows, width = resid_rows.shape
    total_rows = local_rows * 16
    half = total_rows // 2
    rows = half // NWIDE
    factor = 1.0 / math.sqrt(total_rows)

    piece = rows // NZH
    at = (lax.axis_index("c") * 2 + lax.axis_index("zl")) * 4 + lax.axis_index("x")
    block = lax.dynamic_slice_in_dim(resid_rows, at * piece, piece, 0)
    block = (block.astype(f32) - b_decode).astype(bf16)
    block = spread(block, ZH, NZH).reshape(rows, width)
    dec_float = w_decode.astype(f32)
    norms = jnp.sqrt(jnp.sum(dec_float * dec_float, axis=1) + 1e-06)
    slope0 = 0.5 * factor * norms
    block, norms, slope0, slope1, bias1, enc1, dec1 = tie(
        block, norms, slope0, swap(slope0), swap(b_encode), swap(w_encode), swap(w_decode)
    )
    centered = spread(block, WIDE, NWIDE).reshape(half, width)

    def encode(w, b):
        active = jnp.maximum(jnp.dot(centered, w, preferred_element_type=f32) + b, 0.0)
        return active, (active * active).astype(bf16)

    active1, codes1 = encode(enc1, bias1)
    active0, codes0 = encode(w_encode, b_encode)
    part = jnp.dot(codes1, dec1, preferred_element_type=f32) + jnp.dot(
        codes0, w_decode, preferred_element_type=f32
    )
    part = part.astype(bf16).reshape(NWIDE, rows, width)
    part, their_rows, their_codes = tie(part, swap(centered), swap(codes1))
    part = lax.all_to_all(part, WIDE, 0, 0, tiled=True)
    part = jnp.sum(part.astype(f32), axis=0).astype(bf16)
    summed = jnp.sum(spread(part, ZH, NZH).astype(f32), axis=0)
    error_block = (summed - block.astype(f32)).astype(bf16)
    block_sum = 2.0 * factor / NZH * jnp.sum(error_block.astype(f32), axis=0)
    error_block, block_sum = tie(error_block, block_sum)
    error = spread(error_block, WIDE, NWIDE).reshape(half, width)

    def backward(w, slope, active):
        back = 2.0 * factor * jnp.dot(error, w.T, preferred_element_type=f32) + slope
        dpre = back * 2.0 * active
        return dpre.astype(bf16), jnp.sum(dpre, axis=0)

    def times(w, vector):
        first = lax.reduce_precision(vector, 8, 7)
        second = lax.reduce_precision(vector - first, 8, 7)
        third = vector - first - second
        parts = jnp.stack([first, second, third] + [jnp.zeros_like(vector)] * 5).astype(bf16)
        product = lax.dot_general(
            parts, w, (((1,), (1,)), ((), ())), preferred_element_type=f32
        )
        return product[0] + product[1] + product[2]

    dpre1, sums1 = backward(dec1, slope1, active1)
    dpre0, sums0 = backward(w_decode, slope0, active0)
    through = times(w_encode, sums0) + times(enc1, sums1) - block_sum
    through = through.reshape(width // 128, 128)
    through = through + swap(through)

    all_codes = jnp.concatenate([codes0, their_codes], axis=0)
    all_dpre = jnp.concatenate([dpre0, swap(dpre1)], axis=0)
    all_rows = jnp.concatenate([centered, their_rows], axis=0)
    all_error = jnp.concatenate([error, swap(error)], axis=0)
    through, all_codes, all_dpre = tie(through, all_codes, all_dpre)
    code_sum = jnp.sum(all_codes.astype(f32), axis=0)
    through = spread(through, Z, NZ)
    grad_decode = (
        2.0 * factor * jnp.dot(all_codes.T, all_error, preferred_element_type=f32)
        + 0.5 * factor * (code_sum / norms)[:, None] * dec_float
    ).astype(bf16)
    through, grad_decode, all_dpre = tie(through, grad_decode, all_dpre)
    through = jnp.sum(spread(jnp.sum(through, axis=0), XY, NXY), axis=0).reshape(width)
    grad_encode = jnp.dot(all_rows.T, all_dpre, preferred_element_type=f32).astype(bf16)
    grad_b_encode = sums0 + swap(sums1)
    return (grad_encode, grad_b_encode, grad_decode, -through)


def solution(mesh):
    fine = Mesh(mesh.devices.reshape(2, 4, 2, 4, 4), ("zl", "x", "c", "zh", "y"))
    latents = LMAJ + LMIN
    in_specs = (P(LMIN, None), P(None, latents), P(latents), P(latents, None), P())
    out_specs = (P(None, latents), P(latents), P(latents, None), P())
    return jax.shard_map(
        per_device, mesh=fine, in_specs=in_specs, out_specs=out_specs, check_vma=False
    )
```

```python
import functools
import math

import jax
import jax.numpy as jnp
from jax import lax
from jax.experimental import pallas as pl
from jax.experimental.pallas import tpu as pltpu
from jax.sharding import Mesh, PartitionSpec as P

LMAJ = ("zl", "x", "c")
LMIN = ("zh", "y")
WIDE, NWIDE = ("zl", "x", "y"), 32
XY, NXY = ("x", "y"), 16
Z, NZ = ("zl", "zh"), 8
ZH, NZH = ("zh",), 4
f32, bf16 = jnp.float32, jnp.bfloat16
VMEM = pl.BlockSpec(memory_space=pltpu.VMEM)
VMEM_BYTES = 16 * 1024 * 1024
NT = (((1,), (1,)), ((), ()))


def spread(block, axes, n):
    return lax.all_to_all(
        jnp.broadcast_to(block[None], (n,) + block.shape), axes, 0, 0, tiled=True
    )


def swap(block):
    return lax.ppermute(block, "c", [(0, 1), (1, 0)])


def tie(*values):
    return lax.optimization_barrier(values)


def forward_kernel(
    rows, enc0, enc1, dec0, dec1, bias0, bias1, active0, active1, codes0, codes1, part
):
    for enc, bias, active, codes in (
        (enc0, bias0, active0, codes0),
        (enc1, bias1, active1, codes1),
    ):
        pre = jnp.dot(rows[...], enc[...], preferred_element_type=f32) + bias[...]
        value = jnp.maximum(pre, 0.0)
        active[...] = value
        codes[...] = (value * value).astype(bf16)
    total = jnp.dot(codes0[...], dec0[...], preferred_element_type=f32)
    total += jnp.dot(codes1[...], dec1[...], preferred_element_type=f32)
    part[...] = total.astype(bf16)


def forward(rows, enc, dec, bias):
    count, width = rows.shape
    mine = enc[0].shape[1]
    flat = jax.ShapeDtypeStruct((count, mine), f32)
    half = jax.ShapeDtypeStruct((count, mine), bf16)
    return pl.pallas_call(
        forward_kernel,
        out_shape=(flat, flat, half, half, jax.ShapeDtypeStruct((count, width), bf16)),
        in_specs=[VMEM] * 7,
        out_specs=(VMEM,) * 5,
        compiler_params=pltpu.CompilerParams(vmem_limit_bytes=VMEM_BYTES),
        cost_estimate=pl.CostEstimate(
            flops=8 * count * width * mine, bytes_accessed=16_000_000, transcendentals=0
        ),
        name="forward",
    )(rows, *enc, *dec, *bias)


def backward_kernel(
    factor, error, dec0, dec1, enc0, enc1, active0, active1, slope0, slope1, block_sum,
    dpre0, dpre1, sums0, sums1, through,
):
    product = None
    for dec, enc, active, slope, dpre, sums in (
        (dec0, enc0, active0, slope0, dpre0, sums0),
        (dec1, enc1, active1, slope1, dpre1, sums1),
    ):
        back = lax.dot_general(error[...], dec[...], NT, preferred_element_type=f32)
        value = (2.0 * factor * back + slope[...]) * 2.0 * active[...]
        dpre[...] = value.astype(bf16)
        total = jnp.sum(value, axis=0, keepdims=True)
        sums[...] = total
        first = total.astype(bf16)
        rest = total - first.astype(f32)
        second = rest.astype(bf16)
        third = (rest - second.astype(f32)).astype(bf16)
        parts = jnp.concatenate(
            [first, second, third, jnp.zeros((13, total.shape[1]), bf16)], axis=0
        )
        term = lax.dot_general(parts, enc[...], NT, preferred_element_type=f32)
        product = term if product is None else product + term
    row = product[0:1] + product[1:2] + product[2:3]
    for k in range(through.shape[0]):
        through[k : k + 1, :] = row[:, 128 * k : 128 * (k + 1)] - block_sum[k : k + 1, :]


def backward(error, dec, enc, active, slope, block_sum, factor):
    count, width = error.shape
    mine = enc[0].shape[1]
    half = jax.ShapeDtypeStruct((count, mine), bf16)
    line = jax.ShapeDtypeStruct((1, mine), f32)
    return pl.pallas_call(
        functools.partial(backward_kernel, factor),
        out_shape=(half, half, line, line, jax.ShapeDtypeStruct(block_sum.shape, f32)),
        in_specs=[VMEM] * 10,
        out_specs=(VMEM,) * 5,
        compiler_params=pltpu.CompilerParams(vmem_limit_bytes=VMEM_BYTES),
        cost_estimate=pl.CostEstimate(
            flops=6 * count * width * mine, bytes_accessed=15_000_000, transcendentals=0
        ),
        name="backward",
    )(error, *dec, *enc, *active, *slope, block_sum)


def per_device(resid_rows, w_encode, b_encode, w_decode, b_decode):
    local_rows, width = resid_rows.shape
    total_rows = local_rows * 16
    half = total_rows // 2
    rows = half // NWIDE
    factor = 1.0 / math.sqrt(total_rows)

    piece = rows // NZH
    at = (lax.axis_index("c") * 2 + lax.axis_index("zl")) * 4 + lax.axis_index("x")
    block = lax.dynamic_slice_in_dim(resid_rows, at * piece, piece, 0)
    block = (block.astype(f32) - b_decode).astype(bf16)
    block = spread(block, ZH, NZH).reshape(rows, width)
    dec_float = w_decode.astype(f32)
    norms = jnp.sqrt(jnp.sum(dec_float * dec_float, axis=1) + 1e-06)
    slope0 = (0.5 * factor * norms).reshape(1, -1)
    bias0 = b_encode.reshape(1, -1)
    block, norms, slope0, slope1, bias0, bias1, enc1, dec1 = tie(
        block, norms, slope0, swap(slope0), bias0, swap(bias0), swap(w_encode), swap(w_decode)
    )
    centered = spread(block, WIDE, NWIDE).reshape(half, width)

    active0, active1, codes0, codes1, part = forward(
        centered, (w_encode, enc1), (w_decode, dec1), (bias0, bias1)
    )
    part = part.reshape(NWIDE, rows, width)
    part = lax.all_to_all(part, WIDE, 0, 0, tiled=True)
    part = jnp.sum(part.astype(f32), axis=0).astype(bf16)
    summed = jnp.sum(spread(part, ZH, NZH).astype(f32), axis=0)
    error_block = (summed - block.astype(f32)).astype(bf16)
    block_sum = 2.0 * factor / NZH * jnp.sum(error_block.astype(f32), axis=0)
    block_sum = block_sum.reshape(width // 128, 128)
    error_block, block_sum = tie(error_block, block_sum)
    error = spread(error_block, WIDE, NWIDE).reshape(half, width)
    error, centered, codes1 = tie(error, centered, codes1)

    dpre0, dpre1, sums0, sums1, through = backward(
        error, (w_decode, dec1), (w_encode, enc1), (active0, active1), (slope0, slope1),
        block_sum, factor,
    )
    through = through + swap(through)

    all_codes = jnp.concatenate([codes0, swap(codes1)], axis=0)
    all_dpre = jnp.concatenate([dpre0, swap(dpre1)], axis=0)
    all_rows = jnp.concatenate([centered, swap(centered)], axis=0)
    all_error = jnp.concatenate([error, swap(error)], axis=0)
    through, all_codes, all_dpre = tie(through, all_codes, all_dpre)
    code_sum = jnp.sum(all_codes.astype(f32), axis=0)
    through = spread(through, Z, NZ)
    grad_decode = (
        2.0 * factor * jnp.dot(all_codes.T, all_error, preferred_element_type=f32)
        + 0.5 * factor * (code_sum / norms)[:, None] * dec_float
    ).astype(bf16)
    through, grad_decode, all_dpre = tie(through, grad_decode, all_dpre)
    through = jnp.sum(spread(jnp.sum(through, axis=0), XY, NXY), axis=0).reshape(width)
    grad_encode = jnp.dot(all_rows.T, all_dpre, preferred_element_type=f32).astype(bf16)
    grad_b_encode = (sums0 + swap(sums1)).reshape(-1)
    return (grad_encode, grad_b_encode, grad_decode, -through)


def solution(mesh):
    fine = Mesh(mesh.devices.reshape(2, 4, 2, 4, 4), ("zl", "x", "c", "zh", "y"))
    latents = LMAJ + LMIN
    in_specs = (P(LMIN, None), P(None, latents), P(latents), P(latents, None), P())
    out_specs = (P(None, latents), P(latents), P(latents, None), P())
    return jax.shard_map(
        per_device, mesh=fine, in_specs=in_specs, out_specs=out_specs, check_vma=False
    )
```

```python
import functools
import math

import jax
import jax.numpy as jnp
from jax import lax
from jax.experimental import pallas as pl
from jax.experimental.pallas import tpu as pltpu
from jax.sharding import Mesh, PartitionSpec as P

LMAJ = ("zl", "x", "c")
LMIN = ("zh", "y")
WIDE, NWIDE = ("zl", "x", "y"), 32
XY, NXY = ("x", "y"), 16
Z, NZ = ("zl", "zh"), 8
ZH, NZH = ("zh",), 4
f32, bf16 = jnp.float32, jnp.bfloat16
VMEM = pl.BlockSpec(memory_space=pltpu.VMEM)
ANY = pl.BlockSpec(memory_space=pl.ANY)
VMEM_BYTES = 16 * 1024 * 1024
SMALL_BYTES = 6 * 1024 * 1024
NT = (((1,), (1,)), ((), ()))


def spread(block, axes, n):
    return lax.all_to_all(
        jnp.broadcast_to(block[None], (n,) + block.shape), axes, 0, 0, tiled=True
    )


def swap(block):
    return lax.ppermute(block, "c", [(0, 1), (1, 0)])


def tie(*values):
    return lax.optimization_barrier(values)


def small_kernel(body, out_shape, *args, name):
    return pl.pallas_call(
        body,
        out_shape=out_shape,
        in_specs=[VMEM] * len(args),
        out_specs=jax.tree.map(lambda _: VMEM, out_shape),
        compiler_params=pltpu.CompilerParams(vmem_limit_bytes=SMALL_BYTES),
        name=name,
    )(*args)


def repeat_into(out, value):
    for k in range(out.shape[0]):
        out[k] = value


def collect_kernel(pieces, enc_hbm, dec_hbm, block, out, enc, dec, sem):
    copies = (
        pltpu.make_async_copy(enc_hbm, enc, sem.at[0]),
        pltpu.make_async_copy(dec_hbm, dec, sem.at[1]),
    )
    for copy in copies:
        copy.start()
    value = jnp.concatenate([pieces[k] for k in range(pieces.shape[0])], axis=0)
    block[...] = value
    repeat_into(out, value)
    for copy in copies:
        copy.wait()


def collect(pieces, enc, dec, wide):
    count, rows, width = pieces.shape
    return pl.pallas_call(
        collect_kernel,
        out_shape=(
            jax.ShapeDtypeStruct((count * rows, width), bf16),
            jax.ShapeDtypeStruct((wide, count * rows, width), bf16),
            jax.ShapeDtypeStruct(enc.shape, bf16),
            jax.ShapeDtypeStruct(dec.shape, bf16),
        ),
        in_specs=[VMEM, ANY, ANY],
        out_specs=(VMEM,) * 4,
        scratch_shapes=[pltpu.SemaphoreType.DMA((2,))],
        compiler_params=pltpu.CompilerParams(vmem_limit_bytes=SMALL_BYTES),
        name="collect",
    )(pieces, enc, dec)


def reduce_kernel(parts, out):
    total = parts[0].astype(f32)
    for k in range(1, parts.shape[0]):
        total += parts[k].astype(f32)
    repeat_into(out, total.astype(bf16))


def error_kernel(factor, parts, block, out, block_sum):
    total = parts[0].astype(f32)
    for k in range(1, parts.shape[0]):
        total += parts[k].astype(f32)
    error = (total - block[...].astype(f32)).astype(bf16)
    repeat_into(out, error)
    row = (2.0 * factor / parts.shape[0]) * jnp.sum(error.astype(f32), axis=0, keepdims=True)
    for k in range(block_sum.shape[0]):
        block_sum[k : k + 1, :] = row[:, 128 * k : 128 * (k + 1)]


def forward_kernel(
    rows, enc0, enc1, dec0, dec1, bias0, bias1,
    active0, active1, codes0, codes1, part, rows_out, sem,
):
    copy = pltpu.make_async_copy(rows, rows_out, sem)
    copy.start()
    for enc, bias, active, codes in (
        (enc0, bias0, active0, codes0),
        (enc1, bias1, active1, codes1),
    ):
        pre = jnp.dot(rows[...], enc[...], preferred_element_type=f32) + bias[...]
        value = jnp.maximum(pre, 0.0)
        active[...] = value
        codes[...] = (value * value).astype(bf16)
    total = jnp.dot(codes0[...], dec0[...], preferred_element_type=f32)
    total += jnp.dot(codes1[...], dec1[...], preferred_element_type=f32)
    part[...] = total.astype(bf16)
    copy.wait()


def forward(rows, enc, dec, bias):
    count, width = rows.shape
    mine = enc[0].shape[1]
    flat = jax.ShapeDtypeStruct((count, mine), f32)
    half = jax.ShapeDtypeStruct((count, mine), bf16)
    full = jax.ShapeDtypeStruct((count, width), bf16)
    return pl.pallas_call(
        forward_kernel,
        out_shape=(flat, flat, half, half, full, full),
        in_specs=[VMEM] * 7,
        out_specs=(VMEM,) * 5 + (ANY,),
        scratch_shapes=[pltpu.SemaphoreType.DMA],
        compiler_params=pltpu.CompilerParams(vmem_limit_bytes=VMEM_BYTES),
        cost_estimate=pl.CostEstimate(
            flops=8 * count * width * mine, bytes_accessed=16_000_000, transcendentals=0
        ),
        name="forward",
    )(rows, *enc, *dec, *bias)


def backward_kernel(
    factor, error, dec0, dec1, enc0, enc1, active0, active1, slope0, slope1, block_sum,
    dpre0, dpre1, sums0, sums1, through, error_out, sem,
):
    copy = pltpu.make_async_copy(error, error_out, sem)
    copy.start()
    product = None
    for dec, enc, active, slope, dpre, sums in (
        (dec0, enc0, active0, slope0, dpre0, sums0),
        (dec1, enc1, active1, slope1, dpre1, sums1),
    ):
        back = lax.dot_general(error[...], dec[...], NT, preferred_element_type=f32)
        value = (2.0 * factor * back + slope[...]) * 2.0 * active[...]
        dpre[...] = value.astype(bf16)
        total = jnp.sum(value, axis=0, keepdims=True)
        sums[...] = total
        first = total.astype(bf16)
        rest = total - first.astype(f32)
        second = rest.astype(bf16)
        third = (rest - second.astype(f32)).astype(bf16)
        parts = jnp.concatenate(
            [first, second, third, jnp.zeros((13, total.shape[1]), bf16)], axis=0
        )
        term = lax.dot_general(parts, enc[...], NT, preferred_element_type=f32)
        product = term if product is None else product + term
    row = product[0:1] + product[1:2] + product[2:3]
    for k in range(through.shape[0]):
        through[k : k + 1, :] = row[:, 128 * k : 128 * (k + 1)] - block_sum[k : k + 1, :]
    copy.wait()


def backward(error, dec, enc, active, slope, block_sum, factor):
    count, width = error.shape
    mine = enc[0].shape[1]
    half = jax.ShapeDtypeStruct((count, mine), bf16)
    line = jax.ShapeDtypeStruct((1, mine), f32)
    return pl.pallas_call(
        functools.partial(backward_kernel, factor),
        out_shape=(
            half, half, line, line, jax.ShapeDtypeStruct(block_sum.shape, f32),
            jax.ShapeDtypeStruct((count, width), bf16),
        ),
        in_specs=[VMEM] * 10,
        out_specs=(VMEM,) * 5 + (ANY,),
        scratch_shapes=[pltpu.SemaphoreType.DMA],
        compiler_params=pltpu.CompilerParams(vmem_limit_bytes=VMEM_BYTES),
        cost_estimate=pl.CostEstimate(
            flops=6 * count * width * mine, bytes_accessed=15_000_000, transcendentals=0
        ),
        name="backward",
    )(error, *dec, *enc, *active, *slope, block_sum)


def per_device(resid_rows, w_encode, b_encode, w_decode, b_decode):
    local_rows, width = resid_rows.shape
    total_rows = local_rows * 16
    half = total_rows // 2
    rows = half // NWIDE
    factor = 1.0 / math.sqrt(total_rows)

    piece = rows // NZH
    at = (lax.axis_index("c") * 2 + lax.axis_index("zl")) * 4 + lax.axis_index("x")
    block = lax.dynamic_slice_in_dim(resid_rows, at * piece, piece, 0)
    block = (block.astype(f32) - b_decode).astype(bf16)
    pieces = spread(block, ZH, NZH)
    dec_float = w_decode.astype(f32)
    norms = jnp.sqrt(jnp.sum(dec_float * dec_float, axis=1) + 1e-06)
    slope0 = (0.5 * factor * norms).reshape(1, -1)
    bias0 = b_encode.reshape(1, -1)
    pieces, norms, slope0, slope1, bias0, bias1, enc1, dec1 = tie(
        pieces, norms, slope0, swap(slope0), bias0, swap(bias0), swap(w_encode), swap(w_decode)
    )
    wide_shape = jax.ShapeDtypeStruct((NWIDE, rows, width), bf16)
    block, centered, enc1, dec1 = collect(pieces, enc1, dec1, NWIDE)
    centered = lax.all_to_all(centered, WIDE, 0, 0, tiled=True).reshape(half, width)

    active0, active1, codes0, codes1, part, centered = forward(
        centered, (w_encode, enc1), (w_decode, dec1), (bias0, bias1)
    )
    part = part.reshape(NWIDE, rows, width)
    part = lax.all_to_all(part, WIDE, 0, 0, tiled=True)
    part = small_kernel(
        reduce_kernel, jax.ShapeDtypeStruct((NZH, rows, width), bf16), part, name="reduce"
    )
    part = lax.all_to_all(part, ZH, 0, 0, tiled=True)
    error, block_sum = small_kernel(
        functools.partial(error_kernel, factor),
        (wide_shape, jax.ShapeDtypeStruct((width // 128, 128), f32)),
        part, block, name="error",
    )
    error = lax.all_to_all(error, WIDE, 0, 0, tiled=True).reshape(half, width)
    error, centered, codes1 = tie(error, centered, codes1)

    dpre0, dpre1, sums0, sums1, through, error = backward(
        error, (w_decode, dec1), (w_encode, enc1), (active0, active1), (slope0, slope1),
        block_sum, factor,
    )
    through = through + swap(through)

    all_codes = jnp.concatenate([codes0, swap(codes1)], axis=0)
    all_dpre = jnp.concatenate([dpre0, swap(dpre1)], axis=0)
    all_rows = jnp.concatenate([centered, swap(centered)], axis=0)
    all_error = jnp.concatenate([error, swap(error)], axis=0)
    through, all_codes, all_dpre = tie(through, all_codes, all_dpre)
    code_sum = jnp.sum(all_codes.astype(f32), axis=0)
    through = spread(through, Z, NZ)
    grad_decode = (
        2.0 * factor * jnp.dot(all_codes.T, all_error, preferred_element_type=f32)
        + 0.5 * factor * (code_sum / norms)[:, None] * dec_float
    ).astype(bf16)
    through, grad_decode, all_dpre = tie(through, grad_decode, all_dpre)
    through = jnp.sum(spread(jnp.sum(through, axis=0), XY, NXY), axis=0).reshape(width)
    grad_encode = jnp.dot(all_rows.T, all_dpre, preferred_element_type=f32).astype(bf16)
    grad_b_encode = (sums0 + swap(sums1)).reshape(-1)
    return (grad_encode, grad_b_encode, grad_decode, -through)


def solution(mesh):
    fine = Mesh(mesh.devices.reshape(2, 4, 2, 4, 4), ("zl", "x", "c", "zh", "y"))
    latents = LMAJ + LMIN
    in_specs = (P(LMIN, None), P(None, latents), P(latents), P(latents, None), P())
    out_specs = (P(None, latents), P(latents), P(latents, None), P())
    return jax.shard_map(
        per_device, mesh=fine, in_specs=in_specs, out_specs=out_specs, check_vma=False
    )
```

```python
import functools
import math

import jax
import jax.numpy as jnp
from jax import lax
from jax.experimental import pallas as pl
from jax.experimental.pallas import tpu as pltpu
from jax.sharding import Mesh, PartitionSpec as P

LMAJ = ("zl", "x", "c")
LMIN = ("zh", "y")
WIDE, NWIDE = ("zl", "x", "y"), 32
XY, NXY = ("x", "y"), 16
Z, NZ = ("zl", "zh"), 8
ZH, NZH = ("zh",), 4
f32, bf16 = jnp.float32, jnp.bfloat16
VMEM = pl.BlockSpec(memory_space=pltpu.VMEM)
ANY = pl.BlockSpec(memory_space=pl.ANY)
VMEM_BYTES = 16 * 1024 * 1024
SMALL_BYTES = 6 * 1024 * 1024
GRAD_BYTES = 24 * 1024 * 1024
PART = 896
NT = (((1,), (1,)), ((), ()))


def spread(block, axes, n):
    return lax.all_to_all(
        jnp.broadcast_to(block[None], (n,) + block.shape), axes, 0, 0, tiled=True
    )


def swap(block):
    return lax.ppermute(block, "c", [(0, 1), (1, 0)])


def tie(*values):
    return lax.optimization_barrier(values)


def small_kernel(body, out_shape, *args, name):
    return pl.pallas_call(
        body,
        out_shape=out_shape,
        in_specs=[VMEM] * len(args),
        out_specs=jax.tree.map(lambda _: VMEM, out_shape),
        compiler_params=pltpu.CompilerParams(vmem_limit_bytes=SMALL_BYTES),
        name=name,
    )(*args)


def repeat_into(out, value):
    for k in range(out.shape[0]):
        out[k] = value


def collect_kernel(pieces, bias, block, out):
    value = jnp.concatenate([pieces[k] for k in range(pieces.shape[0])], axis=0)
    value = (value.astype(f32) - bias[...]).astype(bf16)
    block[...] = value
    repeat_into(out, value)


def reduce_kernel(parts, out):
    total = parts[0].astype(f32)
    for k in range(1, parts.shape[0]):
        total += parts[k].astype(f32)
    repeat_into(out, total.astype(bf16))


def error_kernel(factor, parts, block, out, block_sum):
    total = parts[0].astype(f32)
    for k in range(1, parts.shape[0]):
        total += parts[k].astype(f32)
    error = (total - block[...].astype(f32)).astype(bf16)
    repeat_into(out, error)
    row = (2.0 * factor / parts.shape[0]) * jnp.sum(error.astype(f32), axis=0, keepdims=True)
    for k in range(block_sum.shape[0]):
        block_sum[k : k + 1, :] = row[:, 128 * k : 128 * (k + 1)]


def forward_kernel(
    rows, enc0, enc1_hbm, dec0, dec1_hbm, bias0, bias1,
    active0, active1, codes0, codes1, part, rows_out, enc1, dec1, sem,
):
    load_enc = pltpu.make_async_copy(enc1_hbm, enc1, sem.at[0])
    load_dec = pltpu.make_async_copy(dec1_hbm, dec1, sem.at[1])
    copy = pltpu.make_async_copy(rows, rows_out, sem.at[2])
    load_enc.start()
    load_dec.start()

    def encode(enc, bias, active, codes):
        pre = jnp.dot(rows[...], enc[...], preferred_element_type=f32) + bias[...]
        value = jnp.maximum(pre, 0.0)
        active[...] = value
        codes[...] = (value * value).astype(bf16)

    encode(enc0, bias0, active0, codes0)
    load_enc.wait()
    encode(enc1, bias1, active1, codes1)
    copy.start()
    load_dec.wait()
    total = jnp.dot(codes0[...], dec0[...], preferred_element_type=f32)
    total += jnp.dot(codes1[...], dec1[...], preferred_element_type=f32)
    part[...] = total.astype(bf16)
    copy.wait()


def forward(rows, enc, dec, bias):
    count, width = rows.shape
    mine = enc[0].shape[1]
    flat = jax.ShapeDtypeStruct((count, mine), f32)
    half = jax.ShapeDtypeStruct((count, mine), bf16)
    full = jax.ShapeDtypeStruct((count, width), bf16)
    weights = (jax.ShapeDtypeStruct(w.shape, bf16) for w in (enc[1], dec[1]))
    return pl.pallas_call(
        forward_kernel,
        out_shape=(flat, flat, half, half, full, full, *weights),
        in_specs=[VMEM, VMEM, ANY, VMEM, ANY, VMEM, VMEM],
        out_specs=(VMEM,) * 5 + (ANY,) + (VMEM,) * 2,
        scratch_shapes=[pltpu.SemaphoreType.DMA((3,))],
        compiler_params=pltpu.CompilerParams(vmem_limit_bytes=VMEM_BYTES),
        cost_estimate=pl.CostEstimate(
            flops=8 * count * width * mine, bytes_accessed=16_000_000, transcendentals=0
        ),
        name="forward",
    )(rows, enc[0], enc[1], dec[0], dec[1], *bias)


def backward_kernel(
    factor, error, dec0, dec1, enc0, enc1, active0, active1, slope0, slope1, block_sum,
    dpre0, dpre1, sums0, sums1, through, error_out, rounded, sem,
):
    copies = [
        pltpu.make_async_copy(rounded.at[0], dpre0, sem.at[0]),
        pltpu.make_async_copy(rounded.at[1], dpre1, sem.at[1]),
        pltpu.make_async_copy(error, error_out, sem.at[2]),
    ]
    product = None
    for k, (dec, enc, active, slope, sums) in enumerate((
        (dec0, enc0, active0, slope0, sums0),
        (dec1, enc1, active1, slope1, sums1),
    )):
        back = lax.dot_general(error[...], dec[...], NT, preferred_element_type=f32)
        value = (2.0 * factor * back + slope[...]) * 2.0 * active[...]
        rounded[k] = value.astype(bf16)
        copies[k].start()
        total = jnp.sum(value, axis=0, keepdims=True)
        sums[...] = total
        first = total.astype(bf16)
        rest = total - first.astype(f32)
        second = rest.astype(bf16)
        third = (rest - second.astype(f32)).astype(bf16)
        parts = jnp.concatenate(
            [first, second, third, jnp.zeros((13, total.shape[1]), bf16)], axis=0
        )
        term = lax.dot_general(parts, enc[...], NT, preferred_element_type=f32)
        product = term if product is None else product + term
    copies[2].start()
    row = product[0:1] + product[1:2] + product[2:3]
    for k in range(through.shape[0]):
        through[k : k + 1, :] = row[:, 128 * k : 128 * (k + 1)] - block_sum[k : k + 1, :]
    for copy in copies:
        copy.wait()


def backward(error, dec, enc, active, slope, block_sum, factor):
    count, width = error.shape
    mine = enc[0].shape[1]
    half = jax.ShapeDtypeStruct((count, mine), bf16)
    line = jax.ShapeDtypeStruct((1, mine), f32)
    return pl.pallas_call(
        functools.partial(backward_kernel, factor),
        out_shape=(
            half, half, line, line, jax.ShapeDtypeStruct(block_sum.shape, f32),
            jax.ShapeDtypeStruct((count, width), bf16),
        ),
        in_specs=[VMEM] * 10,
        out_specs=(ANY,) * 2 + (VMEM,) * 3 + (ANY,),
        scratch_shapes=[pltpu.VMEM((2, count, mine), bf16), pltpu.SemaphoreType.DMA((3,))],
        compiler_params=pltpu.CompilerParams(vmem_limit_bytes=VMEM_BYTES),
        cost_estimate=pl.CostEstimate(
            flops=6 * count * width * mine, bytes_accessed=15_000_000, transcendentals=0
        ),
        name="backward",
    )(error, *dec, *enc, *active, *slope, block_sum)


def decode_grad_kernel(
    factor, codes0, codes1, error0, error1, dec, norms, out,
    codes_in, error_in, dec_in, out_buf, sem_codes, sem_in, sem_out,
):
    half, width = error0.shape
    first = [
        pltpu.make_async_copy(codes0, codes_in.at[:half], sem_codes.at[0]),
        pltpu.make_async_copy(codes1, codes_in.at[half:], sem_codes.at[1]),
    ]
    loads, stores = [], []
    for k in range(width // PART):
        at = slice(k * PART, (k + 1) * PART)
        loads.append((
            pltpu.make_async_copy(error0.at[:, at], error_in.at[:half, at], sem_in.at[0, k]),
            pltpu.make_async_copy(error1.at[:, at], error_in.at[half:, at], sem_in.at[1, k]),
            pltpu.make_async_copy(dec.at[:, at], dec_in.at[:, at], sem_in.at[2, k]),
        ))
        stores.append(pltpu.make_async_copy(out_buf.at[:, at], out.at[:, at], sem_out.at[k]))
    for group in (first, *loads):
        for copy in group:
            copy.start()
    for copy in first:
        copy.wait()
    codes = codes_in[...].T
    norm = jnp.broadcast_to(norms[...], (8, norms.shape[1])).T[:, :1]
    scale = 0.5 * factor * (jnp.sum(codes.astype(f32), axis=1, keepdims=True) / norm)
    for k in range(width // PART):
        at = slice(k * PART, (k + 1) * PART)
        for copy in loads[k]:
            copy.wait()
        grad = 2.0 * factor * jnp.dot(codes, error_in[:, at], preferred_element_type=f32)
        out_buf[:, at] = (grad + scale * dec_in[:, at].astype(f32)).astype(bf16)
        stores[k].start()
    for copy in stores:
        copy.wait()


def decode_grad(codes, error, dec, norms, factor):
    half, width = error[0].shape
    mine = dec.shape[0]
    steps = width // PART
    return pl.pallas_call(
        functools.partial(decode_grad_kernel, factor),
        out_shape=jax.ShapeDtypeStruct((mine, width), bf16),
        in_specs=[ANY] * 5 + [VMEM],
        out_specs=ANY,
        scratch_shapes=[
            pltpu.VMEM((2 * half, mine), bf16),
            pltpu.VMEM((2 * half, width), bf16),
            pltpu.VMEM((mine, width), bf16),
            pltpu.VMEM((mine, width), bf16),
            pltpu.SemaphoreType.DMA((2,)),
            pltpu.SemaphoreType.DMA((3, steps)),
            pltpu.SemaphoreType.DMA((steps,)),
        ],
        compiler_params=pltpu.CompilerParams(vmem_limit_bytes=GRAD_BYTES),
        cost_estimate=pl.CostEstimate(
            flops=4 * half * width * mine, bytes_accessed=10_000_000, transcendentals=0
        ),
        name="decode_grad",
    )(*codes, *error, dec, norms)


def encode_grad_kernel(
    rows0, rows1, dpre0, dpre1, out, rows_in, dpre_in, out_buf, sem_dpre, sem_in, sem_out
):
    half, width = rows0.shape
    first = [
        pltpu.make_async_copy(dpre0, dpre_in.at[:half], sem_dpre.at[0]),
        pltpu.make_async_copy(dpre1, dpre_in.at[half:], sem_dpre.at[1]),
    ]
    loads, stores = [], []
    for k in range(width // PART):
        at = slice(k * PART, (k + 1) * PART)
        loads.append((
            pltpu.make_async_copy(rows0.at[:, at], rows_in.at[:half, at], sem_in.at[0, k]),
            pltpu.make_async_copy(rows1.at[:, at], rows_in.at[half:, at], sem_in.at[1, k]),
        ))
        stores.append(pltpu.make_async_copy(out_buf.at[at], out.at[at], sem_out.at[k]))
    for group in (first, *loads):
        for copy in group:
            copy.start()
    for copy in first:
        copy.wait()
    for k in range(width // PART):
        at = slice(k * PART, (k + 1) * PART)
        for copy in loads[k]:
            copy.wait()
        out_buf[at] = jnp.dot(
            rows_in[:, at].T, dpre_in[...], preferred_element_type=f32
        ).astype(bf16)
        stores[k].start()
    for copy in stores:
        copy.wait()


def encode_grad(rows, dpre):
    half, width = rows[0].shape
    mine = dpre[0].shape[1]
    steps = width // PART
    return pl.pallas_call(
        encode_grad_kernel,
        out_shape=jax.ShapeDtypeStruct((width, mine), bf16),
        in_specs=[ANY] * 4,
        out_specs=ANY,
        scratch_shapes=[
            pltpu.VMEM((2 * half, width), bf16),
            pltpu.VMEM((2 * half, mine), bf16),
            pltpu.VMEM((width, mine), bf16),
            pltpu.SemaphoreType.DMA((2,)),
            pltpu.SemaphoreType.DMA((2, steps)),
            pltpu.SemaphoreType.DMA((steps,)),
        ],
        compiler_params=pltpu.CompilerParams(vmem_limit_bytes=GRAD_BYTES),
        cost_estimate=pl.CostEstimate(
            flops=4 * half * width * mine, bytes_accessed=7_000_000, transcendentals=0
        ),
        name="encode_grad",
    )(*rows, *dpre)


def per_device(resid_rows, w_encode, b_encode, w_decode, b_decode):
    local_rows, width = resid_rows.shape
    total_rows = local_rows * 16
    half = total_rows // 2
    rows = half // NWIDE
    factor = 1.0 / math.sqrt(total_rows)

    piece = rows // NZH
    at = (lax.axis_index("c") * 2 + lax.axis_index("zl")) * 4 + lax.axis_index("x")
    block = lax.dynamic_slice_in_dim(resid_rows, at * piece, piece, 0)
    pieces = spread(block, ZH, NZH)
    dec_float = w_decode.astype(f32)
    norms = jnp.sqrt(jnp.sum(dec_float * dec_float, axis=1) + 1e-06)
    slope0 = (0.5 * factor * norms).reshape(1, -1)
    bias0 = b_encode.reshape(1, -1)
    center = b_decode.reshape(1, -1)
    pieces, center, norms, slope0, slope1, bias0, bias1, enc1, dec1 = tie(
        pieces, center, norms.reshape(1, -1), slope0, swap(slope0), bias0, swap(bias0),
        swap(w_encode), swap(w_decode),
    )
    wide_shape = jax.ShapeDtypeStruct((NWIDE, rows, width), bf16)
    block_shape = jax.ShapeDtypeStruct((rows, width), bf16)
    block, centered = small_kernel(
        collect_kernel, (block_shape, wide_shape), pieces, center, name="collect"
    )
    centered = lax.all_to_all(centered, WIDE, 0, 0, tiled=True).reshape(half, width)

    active0, active1, codes0, codes1, part, centered, enc1, dec1 = forward(
        centered, (w_encode, enc1), (w_decode, dec1), (bias0, bias1)
    )
    part = part.reshape(NWIDE, rows, width)
    part = lax.all_to_all(part, WIDE, 0, 0, tiled=True)
    part = small_kernel(
        reduce_kernel, jax.ShapeDtypeStruct((NZH, rows, width), bf16), part, name="reduce"
    )
    part = lax.all_to_all(part, ZH, 0, 0, tiled=True)
    error, block_sum = small_kernel(
        functools.partial(error_kernel, factor),
        (wide_shape, jax.ShapeDtypeStruct((width // 128, 128), f32)),
        part, block, name="error",
    )
    error = lax.all_to_all(error, WIDE, 0, 0, tiled=True).reshape(half, width)
    dpre0, dpre1, sums0, sums1, through, error = backward(
        error, (w_decode, dec1), (w_encode, enc1), (active0, active1), (slope0, slope1),
        block_sum, factor,
    )
    through = through + swap(through)
    their_dpre = swap(dpre1)
    through, centered, error, codes1, sums1 = tie(through, centered, error, codes1, sums1)
    their_codes = swap(codes1)
    their_error, their_rows = swap(error), swap(centered)
    through = spread(through, Z, NZ)
    grad_decode = decode_grad(
        (codes0, their_codes), (error, their_error), w_decode, norms, factor
    )
    through, grad_decode, their_dpre = tie(through, grad_decode, their_dpre)
    through = jnp.sum(spread(jnp.sum(through, axis=0), XY, NXY), axis=0).reshape(width)
    grad_encode = encode_grad((centered, their_rows), (dpre0, their_dpre))
    grad_b_encode = (sums0 + swap(sums1)).reshape(-1)
    return (grad_encode, grad_b_encode, grad_decode, -through)


def solution(mesh):
    fine = Mesh(mesh.devices.reshape(2, 4, 2, 4, 4), ("zl", "x", "c", "zh", "y"))
    latents = LMAJ + LMIN
    in_specs = (P(LMIN, None), P(None, latents), P(latents), P(latents, None), P())
    out_specs = (P(None, latents), P(latents), P(latents, None), P())
    return jax.shard_map(
        per_device, mesh=fine, in_specs=in_specs, out_specs=out_specs, check_vma=False
    )
```

```python
import functools
import math

import jax
import jax.numpy as jnp
from jax import lax
from jax.experimental import pallas as pl
from jax.experimental.pallas import tpu as pltpu
from jax.sharding import Mesh, PartitionSpec as P

LMAJ = ("zl", "x", "c")
LMIN = ("zh", "y")
WIDE, NWIDE = ("zl", "x", "y"), 32
XY, NXY = ("x", "y"), 16
Z, NZ = ("zl", "zh"), 8
ZH, NZH = ("zh",), 4
f32, bf16 = jnp.float32, jnp.bfloat16
VMEM = pl.BlockSpec(memory_space=pltpu.VMEM)
HBM = pl.BlockSpec(memory_space=pl.ANY)
VMEM_BYTES = 16 * 1024 * 1024
SMALL_BYTES = 6 * 1024 * 1024
GRAD_BYTES = 24 * 1024 * 1024
PART = 896
ENC_PIECE = 448
DEC_PIECE = 48
NT = (((1,), (1,)), ((), ()))


def spread(block, axes, n):
    return lax.all_to_all(
        jnp.broadcast_to(block[None], (n,) + block.shape), axes, 0, 0, tiled=True
    )


def swap(block):
    return lax.ppermute(block, "c", [(0, 1), (1, 0)])


def tie(*values):
    return lax.optimization_barrier(values)


def small_kernel(body, out_shape, *args, name):
    return pl.pallas_call(
        body,
        out_shape=out_shape,
        in_specs=[VMEM] * len(args),
        out_specs=jax.tree.map(lambda _: VMEM, out_shape),
        compiler_params=pltpu.CompilerParams(vmem_limit_bytes=SMALL_BYTES),
        name=name,
    )(*args)


def repeat_into(out, value):
    for k in range(out.shape[0]):
        out[k] = value


def collect_kernel(pieces, bias, enc_hbm, dec_hbm, block, out, enc, dec, sem):
    first = lax.axis_index("c") == 0

    def load(source, to, rows, k):
        at = pl.ds(pl.multiple_of(k * rows, rows), rows)
        copy = pltpu.make_async_copy(source.at[at], to.at[at], sem.at[0])
        copy.start()
        copy.wait()

    @pl.when(first)
    def _():
        pl.loop(0, enc.shape[0] // ENC_PIECE)(functools.partial(load, enc_hbm, enc, ENC_PIECE))
        pl.loop(0, dec.shape[0] // DEC_PIECE)(functools.partial(load, dec_hbm, dec, DEC_PIECE))

    @pl.when(jnp.logical_not(first))
    def _():
        copies = (
            pltpu.make_async_copy(enc_hbm, enc, sem.at[0]),
            pltpu.make_async_copy(dec_hbm, dec, sem.at[1]),
        )
        for copy in copies:
            copy.start()
        for copy in copies:
            copy.wait()

    value = jnp.concatenate([pieces[k] for k in range(pieces.shape[0])], axis=0)
    value = (value.astype(f32) - bias[...]).astype(bf16)
    block[...] = value
    repeat_into(out, value)


def collect(pieces, bias, enc, dec, wide):
    count, rows, width = pieces.shape
    return pl.pallas_call(
        collect_kernel,
        out_shape=(
            jax.ShapeDtypeStruct((count * rows, width), bf16),
            jax.ShapeDtypeStruct((wide, count * rows, width), bf16),
            jax.ShapeDtypeStruct(enc.shape, bf16),
            jax.ShapeDtypeStruct(dec.shape, bf16),
        ),
        in_specs=[VMEM, VMEM, HBM, HBM],
        out_specs=(VMEM,) * 4,
        scratch_shapes=[pltpu.SemaphoreType.DMA((2,))],
        compiler_params=pltpu.CompilerParams(vmem_limit_bytes=SMALL_BYTES),
        name="collect",
    )(pieces, bias, enc, dec)


def reduce_kernel(parts, out):
    total = parts[0].astype(f32)
    for k in range(1, parts.shape[0]):
        total += parts[k].astype(f32)
    repeat_into(out, total.astype(bf16))


def error_kernel(factor, parts, block, out, block_sum):
    total = parts[0].astype(f32)
    for k in range(1, parts.shape[0]):
        total += parts[k].astype(f32)
    error = (total - block[...].astype(f32)).astype(bf16)
    repeat_into(out, error)
    row = (2.0 * factor / parts.shape[0]) * jnp.sum(error.astype(f32), axis=0, keepdims=True)
    for k in range(block_sum.shape[0]):
        block_sum[k : k + 1, :] = row[:, 128 * k : 128 * (k + 1)]


def forward_kernel(
    rows, enc0, enc1, dec0, dec1, bias0, bias1,
    active0, active1, codes0, codes1, part, rows_out, sem,
):
    copy = pltpu.make_async_copy(rows, rows_out, sem)
    copy.start()
    for enc, bias, active, codes in (
        (enc0, bias0, active0, codes0),
        (enc1, bias1, active1, codes1),
    ):
        pre = jnp.dot(rows[...], enc[...], preferred_element_type=f32) + bias[...]
        value = jnp.maximum(pre, 0.0)
        active[...] = value
        codes[...] = (value * value).astype(bf16)
    total = jnp.dot(codes0[...], dec0[...], preferred_element_type=f32)
    total += jnp.dot(codes1[...], dec1[...], preferred_element_type=f32)
    part[...] = total.astype(bf16)
    copy.wait()


def forward(rows, enc, dec, bias):
    count, width = rows.shape
    mine = enc[0].shape[1]
    flat = jax.ShapeDtypeStruct((count, mine), f32)
    half = jax.ShapeDtypeStruct((count, mine), bf16)
    full = jax.ShapeDtypeStruct((count, width), bf16)
    return pl.pallas_call(
        forward_kernel,
        out_shape=(flat, flat, half, half, full, full),
        in_specs=[VMEM] * 7,
        out_specs=(VMEM,) * 5 + (HBM,),
        scratch_shapes=[pltpu.SemaphoreType.DMA],
        compiler_params=pltpu.CompilerParams(vmem_limit_bytes=VMEM_BYTES),
        cost_estimate=pl.CostEstimate(
            flops=8 * count * width * mine, bytes_accessed=16_000_000, transcendentals=0
        ),
        name="forward",
    )(rows, *enc, *dec, *bias)


def backward_kernel(
    factor, error, dec0, dec1, enc0, enc1, active0, active1, slope0, slope1, block_sum,
    dpre0, dpre1, sums0, sums1, through, error_out, rounded, sem,
):
    copies = [
        pltpu.make_async_copy(rounded.at[0], dpre0, sem.at[0]),
        pltpu.make_async_copy(rounded.at[1], dpre1, sem.at[1]),
        pltpu.make_async_copy(error, error_out, sem.at[2]),
    ]
    product = None
    for k, (dec, enc, active, slope, sums) in enumerate((
        (dec0, enc0, active0, slope0, sums0),
        (dec1, enc1, active1, slope1, sums1),
    )):
        back = lax.dot_general(error[...], dec[...], NT, preferred_element_type=f32)
        value = (2.0 * factor * back + slope[...]) * 2.0 * active[...]
        rounded[k] = value.astype(bf16)
        copies[k].start()
        total = jnp.sum(value, axis=0, keepdims=True)
        sums[...] = total
        first = total.astype(bf16)
        rest = total - first.astype(f32)
        second = rest.astype(bf16)
        third = (rest - second.astype(f32)).astype(bf16)
        parts = jnp.concatenate(
            [first, second, third, jnp.zeros((13, total.shape[1]), bf16)], axis=0
        )
        term = lax.dot_general(parts, enc[...], NT, preferred_element_type=f32)
        product = term if product is None else product + term
    copies[2].start()
    row = product[0:1] + product[1:2] + product[2:3]
    for k in range(through.shape[0]):
        through[k : k + 1, :] = row[:, 128 * k : 128 * (k + 1)] - block_sum[k : k + 1, :]
    for copy in copies:
        copy.wait()


def backward(error, dec, enc, active, slope, block_sum, factor):
    count, width = error.shape
    mine = enc[0].shape[1]
    half = jax.ShapeDtypeStruct((count, mine), bf16)
    line = jax.ShapeDtypeStruct((1, mine), f32)
    return pl.pallas_call(
        functools.partial(backward_kernel, factor),
        out_shape=(
            half, half, line, line, jax.ShapeDtypeStruct(block_sum.shape, f32),
            jax.ShapeDtypeStruct((count, width), bf16),
        ),
        in_specs=[VMEM] * 10,
        out_specs=(HBM,) * 2 + (VMEM,) * 3 + (HBM,),
        scratch_shapes=[pltpu.VMEM((2, count, mine), bf16), pltpu.SemaphoreType.DMA((3,))],
        compiler_params=pltpu.CompilerParams(vmem_limit_bytes=VMEM_BYTES),
        cost_estimate=pl.CostEstimate(
            flops=6 * count * width * mine, bytes_accessed=15_000_000, transcendentals=0
        ),
        name="backward",
    )(error, *dec, *enc, *active, *slope, block_sum)


def decode_grad_kernel(
    factor, codes0, codes1, error0, error1, dec, norms, out,
    codes_in, error_in, dec_in, out_buf, sem_codes, sem_in, sem_out,
):
    half, width = error0.shape
    first = [
        pltpu.make_async_copy(codes0, codes_in.at[:half], sem_codes.at[0]),
        pltpu.make_async_copy(codes1, codes_in.at[half:], sem_codes.at[1]),
    ]
    loads, stores = [], []
    for k in range(width // PART):
        at = slice(k * PART, (k + 1) * PART)
        loads.append((
            pltpu.make_async_copy(error0.at[:, at], error_in.at[:half, at], sem_in.at[0, k]),
            pltpu.make_async_copy(error1.at[:, at], error_in.at[half:, at], sem_in.at[1, k]),
            pltpu.make_async_copy(dec.at[:, at], dec_in.at[:, at], sem_in.at[2, k]),
        ))
        stores.append(pltpu.make_async_copy(out_buf.at[:, at], out.at[:, at], sem_out.at[k]))
    for group in (first, *loads):
        for copy in group:
            copy.start()
    for copy in first:
        copy.wait()
    codes = codes_in[...].T
    norm = jnp.broadcast_to(norms[...], (8, norms.shape[1])).T[:, :1]
    scale = 0.5 * factor * (jnp.sum(codes.astype(f32), axis=1, keepdims=True) / norm)
    for k in range(width // PART):
        at = slice(k * PART, (k + 1) * PART)
        for copy in loads[k]:
            copy.wait()
        grad = 2.0 * factor * jnp.dot(codes, error_in[:, at], preferred_element_type=f32)
        out_buf[:, at] = (grad + scale * dec_in[:, at].astype(f32)).astype(bf16)
        stores[k].start()
    for copy in stores:
        copy.wait()


def decode_grad(codes, error, dec, norms, factor):
    half, width = error[0].shape
    mine = dec.shape[0]
    steps = width // PART
    return pl.pallas_call(
        functools.partial(decode_grad_kernel, factor),
        out_shape=jax.ShapeDtypeStruct((mine, width), bf16),
        in_specs=[HBM] * 5 + [VMEM],
        out_specs=HBM,
        scratch_shapes=[
            pltpu.VMEM((2 * half, mine), bf16),
            pltpu.VMEM((2 * half, width), bf16),
            pltpu.VMEM((mine, width), bf16),
            pltpu.VMEM((mine, width), bf16),
            pltpu.SemaphoreType.DMA((2,)),
            pltpu.SemaphoreType.DMA((3, steps)),
            pltpu.SemaphoreType.DMA((steps,)),
        ],
        compiler_params=pltpu.CompilerParams(vmem_limit_bytes=GRAD_BYTES),
        cost_estimate=pl.CostEstimate(
            flops=4 * half * width * mine, bytes_accessed=10_000_000, transcendentals=0
        ),
        name="decode_grad",
    )(*codes, *error, dec, norms)


def encode_grad_kernel(
    rows0, rows1, dpre0, dpre1, out, rows_in, dpre_in, out_buf, sem_dpre, sem_in, sem_out
):
    half, width = rows0.shape
    first = [
        pltpu.make_async_copy(dpre0, dpre_in.at[:half], sem_dpre.at[0]),
        pltpu.make_async_copy(dpre1, dpre_in.at[half:], sem_dpre.at[1]),
    ]
    loads, stores = [], []
    for k in range(width // PART):
        at = slice(k * PART, (k + 1) * PART)
        loads.append((
            pltpu.make_async_copy(rows0.at[:, at], rows_in.at[:half, at], sem_in.at[0, k]),
            pltpu.make_async_copy(rows1.at[:, at], rows_in.at[half:, at], sem_in.at[1, k]),
        ))
        stores.append(pltpu.make_async_copy(out_buf.at[at], out.at[at], sem_out.at[k]))
    for group in (first, *loads):
        for copy in group:
            copy.start()
    for copy in first:
        copy.wait()
    for k in range(width // PART):
        at = slice(k * PART, (k + 1) * PART)
        for copy in loads[k]:
            copy.wait()
        out_buf[at] = jnp.dot(
            rows_in[:, at].T, dpre_in[...], preferred_element_type=f32
        ).astype(bf16)
        stores[k].start()
    for copy in stores:
        copy.wait()


def encode_grad(rows, dpre):
    half, width = rows[0].shape
    mine = dpre[0].shape[1]
    steps = width // PART
    return pl.pallas_call(
        encode_grad_kernel,
        out_shape=jax.ShapeDtypeStruct((width, mine), bf16),
        in_specs=[HBM] * 4,
        out_specs=HBM,
        scratch_shapes=[
            pltpu.VMEM((2 * half, width), bf16),
            pltpu.VMEM((2 * half, mine), bf16),
            pltpu.VMEM((width, mine), bf16),
            pltpu.SemaphoreType.DMA((2,)),
            pltpu.SemaphoreType.DMA((2, steps)),
            pltpu.SemaphoreType.DMA((steps,)),
        ],
        compiler_params=pltpu.CompilerParams(vmem_limit_bytes=GRAD_BYTES),
        cost_estimate=pl.CostEstimate(
            flops=4 * half * width * mine, bytes_accessed=7_000_000, transcendentals=0
        ),
        name="encode_grad",
    )(*rows, *dpre)


def per_device(resid_rows, w_encode, b_encode, w_decode, b_decode):
    local_rows, width = resid_rows.shape
    total_rows = local_rows * 16
    half = total_rows // 2
    rows = half // NWIDE
    factor = 1.0 / math.sqrt(total_rows)

    piece = rows // NZH
    at = (lax.axis_index("c") * 2 + lax.axis_index("zl")) * 4 + lax.axis_index("x")
    block = lax.dynamic_slice_in_dim(resid_rows, at * piece, piece, 0)
    pieces = spread(block, ZH, NZH)
    dec_float = w_decode.astype(f32)
    norms = jnp.sqrt(jnp.sum(dec_float * dec_float, axis=1) + 1e-06)
    slope0 = (0.5 * factor * norms).reshape(1, -1)
    bias0 = b_encode.reshape(1, -1)
    center = b_decode.reshape(1, -1)
    pieces, center, norms, slope0, slope1, bias0, bias1, enc1, dec1 = tie(
        pieces, center, norms.reshape(1, -1), slope0, swap(slope0), bias0, swap(bias0),
        swap(w_encode), swap(w_decode),
    )
    wide_shape = jax.ShapeDtypeStruct((NWIDE, rows, width), bf16)
    block, centered, enc1, dec1 = collect(pieces, center, enc1, dec1, NWIDE)
    centered = lax.all_to_all(centered, WIDE, 0, 0, tiled=True).reshape(half, width)

    active0, active1, codes0, codes1, part, centered = forward(
        centered, (w_encode, enc1), (w_decode, dec1), (bias0, bias1)
    )
    part = part.reshape(NWIDE, rows, width)
    part = lax.all_to_all(part, WIDE, 0, 0, tiled=True)
    part = small_kernel(
        reduce_kernel, jax.ShapeDtypeStruct((NZH, rows, width), bf16), part, name="reduce"
    )
    part = lax.all_to_all(part, ZH, 0, 0, tiled=True)
    error, block_sum = small_kernel(
        functools.partial(error_kernel, factor),
        (wide_shape, jax.ShapeDtypeStruct((width // 128, 128), f32)),
        part, block, name="error",
    )
    error = lax.all_to_all(error, WIDE, 0, 0, tiled=True).reshape(half, width)
    dpre0, dpre1, sums0, sums1, through, error = backward(
        error, (w_decode, dec1), (w_encode, enc1), (active0, active1), (slope0, slope1),
        block_sum, factor,
    )
    through = through + swap(through)
    their_dpre = swap(dpre1)
    through, centered, error, codes1, sums1 = tie(through, centered, error, codes1, sums1)
    their_codes = swap(codes1)
    their_error, their_rows = swap(error), swap(centered)
    through = spread(through, Z, NZ)
    grad_decode = decode_grad(
        (codes0, their_codes), (error, their_error), w_decode, norms, factor
    )
    through, grad_decode, their_dpre = tie(through, grad_decode, their_dpre)
    through = jnp.sum(spread(jnp.sum(through, axis=0), XY, NXY), axis=0).reshape(width)
    grad_encode = encode_grad((centered, their_rows), (dpre0, their_dpre))
    grad_b_encode = (sums0 + swap(sums1)).reshape(-1)
    return (grad_encode, grad_b_encode, grad_decode, -through)


def solution(mesh):
    fine = Mesh(mesh.devices.reshape(2, 4, 2, 4, 4), ("zl", "x", "c", "zh", "y"))
    latents = LMAJ + LMIN
    in_specs = (P(LMIN, None), P(None, latents), P(latents), P(latents, None), P())
    out_specs = (P(None, latents), P(latents), P(latents, None), P())
    return jax.shard_map(
        per_device, mesh=fine, in_specs=in_specs, out_specs=out_specs, check_vma=False
    )
```

```python
import functools
import math

import jax
import jax.numpy as jnp
from jax import lax
from jax.experimental import pallas as pl
from jax.experimental.pallas import tpu as pltpu
from jax.sharding import Mesh, PartitionSpec as P

LMAJ = ("zl", "x", "c")
LMIN = ("zh", "y")
WIDE, NWIDE = ("zl", "x", "y"), 32
XY, NXY = ("x", "y"), 16
Z, NZ = ("zl", "zh"), 8
ZH, NZH = ("zh",), 4
f32, bf16 = jnp.float32, jnp.bfloat16
VMEM = pl.BlockSpec(memory_space=pltpu.VMEM)
HBM = pl.BlockSpec(memory_space=pl.ANY)
VMEM_BYTES = 16 * 1024 * 1024
SMALL_BYTES = 6 * 1024 * 1024
GRAD_BYTES = 24 * 1024 * 1024
PART = 896
ENC_PIECE = 448
DEC_PIECE = 48
NT = (((1,), (1,)), ((), ()))


def spread(block, axes, n):
    return lax.all_to_all(
        jnp.broadcast_to(block[None], (n,) + block.shape), axes, 0, 0, tiled=True
    )


def swap(block):
    return lax.ppermute(block, "c", [(0, 1), (1, 0)])


def tie(*values):
    return lax.optimization_barrier(values)


def small_kernel(body, out_shape, *args, name):
    return pl.pallas_call(
        body,
        out_shape=out_shape,
        in_specs=[VMEM] * len(args),
        out_specs=jax.tree.map(lambda _: VMEM, out_shape),
        compiler_params=pltpu.CompilerParams(vmem_limit_bytes=SMALL_BYTES),
        name=name,
    )(*args)


def repeat_into(out, value):
    for k in range(out.shape[0]):
        out[k] = value


def collect_kernel(pieces, bias, enc_hbm, dec_hbm, block, out, enc, dec, sem):
    first = lax.axis_index("c") == 0

    def load(source, to, rows, k):
        at = pl.ds(pl.multiple_of(k * rows, rows), rows)
        copy = pltpu.make_async_copy(source.at[at], to.at[at], sem.at[0])
        copy.start()
        copy.wait()

    @pl.when(first)
    def _():
        pl.loop(0, enc.shape[0] // ENC_PIECE)(functools.partial(load, enc_hbm, enc, ENC_PIECE))
        pl.loop(0, dec.shape[0] // DEC_PIECE)(functools.partial(load, dec_hbm, dec, DEC_PIECE))

    @pl.when(jnp.logical_not(first))
    def _():
        copies = (
            pltpu.make_async_copy(enc_hbm, enc, sem.at[0]),
            pltpu.make_async_copy(dec_hbm, dec, sem.at[1]),
        )
        for copy in copies:
            copy.start()
        for copy in copies:
            copy.wait()

    value = jnp.concatenate([pieces[k] for k in range(pieces.shape[0])], axis=0)
    value = (value.astype(f32) - bias[...]).astype(bf16)
    block[...] = value
    repeat_into(out, value)


def collect(pieces, bias, enc, dec, wide):
    count, rows, width = pieces.shape
    return pl.pallas_call(
        collect_kernel,
        out_shape=(
            jax.ShapeDtypeStruct((count * rows, width), bf16),
            jax.ShapeDtypeStruct((wide, count * rows, width), bf16),
            jax.ShapeDtypeStruct(enc.shape, bf16),
            jax.ShapeDtypeStruct(dec.shape, bf16),
        ),
        in_specs=[VMEM, VMEM, HBM, HBM],
        out_specs=(VMEM,) * 4,
        scratch_shapes=[pltpu.SemaphoreType.DMA((2,))],
        compiler_params=pltpu.CompilerParams(vmem_limit_bytes=SMALL_BYTES),
        name="collect",
    )(pieces, bias, enc, dec)


def reduce_kernel(parts, out):
    total = parts[0].astype(f32)
    for k in range(1, parts.shape[0]):
        total += parts[k].astype(f32)
    repeat_into(out, total.astype(bf16))


def error_kernel(factor, parts, block, out, block_sum):
    total = parts[0].astype(f32)
    for k in range(1, parts.shape[0]):
        total += parts[k].astype(f32)
    error = (total - block[...].astype(f32)).astype(bf16)
    repeat_into(out, error)
    row = (2.0 * factor / parts.shape[0]) * jnp.sum(error.astype(f32), axis=0, keepdims=True)
    for k in range(block_sum.shape[0]):
        block_sum[k : k + 1, :] = row[:, 128 * k : 128 * (k + 1)]


def forward_kernel(
    rows, enc0, enc1, dec0, dec1, bias0, bias1,
    active0, active1, codes0_out, codes1_out, part, rows_out, codes0, codes1, sem,
):
    copies = [
        pltpu.make_async_copy(codes0, codes0_out, sem.at[0]),
        pltpu.make_async_copy(codes1, codes1_out, sem.at[1]),
        pltpu.make_async_copy(rows, rows_out, sem.at[2]),
    ]
    copies[2].start()
    for k, (enc, bias, active, codes) in enumerate((
        (enc0, bias0, active0, codes0),
        (enc1, bias1, active1, codes1),
    )):
        pre = jnp.dot(rows[...], enc[...], preferred_element_type=f32) + bias[...]
        value = jnp.maximum(pre, 0.0)
        active[...] = value
        codes[...] = (value * value).astype(bf16)
        copies[k].start()
    total = jnp.dot(codes0[...], dec0[...], preferred_element_type=f32)
    total += jnp.dot(codes1[...], dec1[...], preferred_element_type=f32)
    part[...] = total.astype(bf16)
    for copy in copies:
        copy.wait()


def forward(rows, enc, dec, bias):
    count, width = rows.shape
    mine = enc[0].shape[1]
    flat = jax.ShapeDtypeStruct((count, mine), f32)
    half = jax.ShapeDtypeStruct((count, mine), bf16)
    full = jax.ShapeDtypeStruct((count, width), bf16)
    return pl.pallas_call(
        forward_kernel,
        out_shape=(flat, flat, half, half, full, full),
        in_specs=[VMEM] * 7,
        out_specs=(VMEM, VMEM, HBM, HBM, VMEM, HBM),
        scratch_shapes=[
            pltpu.VMEM((count, mine), bf16),
            pltpu.VMEM((count, mine), bf16),
            pltpu.SemaphoreType.DMA((3,)),
        ],
        compiler_params=pltpu.CompilerParams(vmem_limit_bytes=VMEM_BYTES),
        cost_estimate=pl.CostEstimate(
            flops=8 * count * width * mine, bytes_accessed=16_000_000, transcendentals=0
        ),
        name="forward",
    )(rows, *enc, *dec, *bias)


def backward_kernel(
    factor, error, dec0, dec1, enc0, enc1, active0, active1, slope0, slope1, block_sum,
    sums0, sums1, through, out, rounded, sem,
):
    width, mine = error.shape[1], rounded.shape[2]
    copies = [
        pltpu.make_async_copy(rounded.at[0], out.at[:, width : width + mine], sem.at[0]),
        pltpu.make_async_copy(rounded.at[1], out.at[:, width + mine :], sem.at[1]),
        pltpu.make_async_copy(error, out.at[:, :width], sem.at[2]),
    ]
    copies[2].start()
    product = None
    for k, (dec, enc, active, slope, sums) in enumerate((
        (dec0, enc0, active0, slope0, sums0),
        (dec1, enc1, active1, slope1, sums1),
    )):
        back = lax.dot_general(error[...], dec[...], NT, preferred_element_type=f32)
        value = (2.0 * factor * back + slope[...]) * 2.0 * active[...]
        rounded[k] = value.astype(bf16)
        copies[k].start()
        total = jnp.sum(value, axis=0, keepdims=True)
        sums[...] = total
        first = total.astype(bf16)
        rest = total - first.astype(f32)
        second = rest.astype(bf16)
        third = (rest - second.astype(f32)).astype(bf16)
        parts = jnp.concatenate(
            [first, second, third, jnp.zeros((13, total.shape[1]), bf16)], axis=0
        )
        term = lax.dot_general(parts, enc[...], NT, preferred_element_type=f32)
        product = term if product is None else product + term
    row = product[0:1] + product[1:2] + product[2:3]
    for k in range(through.shape[0]):
        through[k : k + 1, :] = row[:, 128 * k : 128 * (k + 1)] - block_sum[k : k + 1, :]
    for copy in copies:
        copy.wait()


def backward(error, dec, enc, active, slope, block_sum, factor):
    count, width = error.shape
    mine = enc[0].shape[1]
    line = jax.ShapeDtypeStruct((1, mine), f32)
    return pl.pallas_call(
        functools.partial(backward_kernel, factor),
        out_shape=(
            line, line, jax.ShapeDtypeStruct(block_sum.shape, f32),
            jax.ShapeDtypeStruct((count, width + 2 * mine), bf16),
        ),
        in_specs=[VMEM] * 10,
        out_specs=(VMEM,) * 3 + (HBM,),
        scratch_shapes=[pltpu.VMEM((2, count, mine), bf16), pltpu.SemaphoreType.DMA((3,))],
        compiler_params=pltpu.CompilerParams(vmem_limit_bytes=VMEM_BYTES),
        cost_estimate=pl.CostEstimate(
            flops=6 * count * width * mine, bytes_accessed=15_000_000, transcendentals=0
        ),
        name="backward",
    )(error, *dec, *enc, *active, *slope, block_sum)


def decode_grad_kernel(
    factor, codes0, codes1, error0, error1, dec, norms, out,
    codes_in, error_in, dec_in, out_buf, sem_codes, sem_in, sem_out,
):
    half, width = error0.shape[0], dec.shape[1]
    first = [
        pltpu.make_async_copy(codes0, codes_in.at[:half], sem_codes.at[0]),
        pltpu.make_async_copy(codes1, codes_in.at[half:], sem_codes.at[1]),
    ]
    loads, stores = [], []
    for k in range(width // PART):
        at = slice(k * PART, (k + 1) * PART)
        loads.append((
            pltpu.make_async_copy(error0.at[:, at], error_in.at[:half, at], sem_in.at[0, k]),
            pltpu.make_async_copy(error1.at[:, at], error_in.at[half:, at], sem_in.at[1, k]),
            pltpu.make_async_copy(dec.at[:, at], dec_in.at[:, at], sem_in.at[2, k]),
        ))
        stores.append(pltpu.make_async_copy(out_buf.at[:, at], out.at[:, at], sem_out.at[k]))
    for group in (first, *loads):
        for copy in group:
            copy.start()
    for copy in first:
        copy.wait()
    codes = codes_in[...].T
    norm = jnp.broadcast_to(norms[...], (8, norms.shape[1])).T[:, :1]
    scale = 0.5 * factor * (jnp.sum(codes.astype(f32), axis=1, keepdims=True) / norm)
    for k in range(width // PART):
        at = slice(k * PART, (k + 1) * PART)
        for copy in loads[k]:
            copy.wait()
        grad = 2.0 * factor * jnp.dot(codes, error_in[:, at], preferred_element_type=f32)
        out_buf[:, at] = (grad + scale * dec_in[:, at].astype(f32)).astype(bf16)
        stores[k].start()
    for copy in stores:
        copy.wait()


def decode_grad(codes, error, dec, norms, factor):
    half = error[0].shape[0]
    mine, width = dec.shape
    steps = width // PART
    return pl.pallas_call(
        functools.partial(decode_grad_kernel, factor),
        out_shape=jax.ShapeDtypeStruct((mine, width), bf16),
        in_specs=[HBM] * 5 + [VMEM],
        out_specs=HBM,
        scratch_shapes=[
            pltpu.VMEM((2 * half, mine), bf16),
            pltpu.VMEM((2 * half, width), bf16),
            pltpu.VMEM((mine, width), bf16),
            pltpu.VMEM((mine, width), bf16),
            pltpu.SemaphoreType.DMA((2,)),
            pltpu.SemaphoreType.DMA((3, steps)),
            pltpu.SemaphoreType.DMA((steps,)),
        ],
        compiler_params=pltpu.CompilerParams(vmem_limit_bytes=GRAD_BYTES),
        cost_estimate=pl.CostEstimate(
            flops=4 * half * width * mine, bytes_accessed=10_000_000, transcendentals=0
        ),
        name="decode_grad",
    )(*codes, *error, dec, norms)


def encode_grad_kernel(
    rows0, rows1, error0, error1, out, rows_in, dpre_in, out_buf, sem_dpre, sem_in, sem_out
):
    half, width = rows0.shape
    mine = out.shape[1]
    dpre0 = error0.at[:, width : width + mine]
    dpre1 = error1.at[:, width + mine :]
    first = [
        pltpu.make_async_copy(dpre0, dpre_in.at[:half], sem_dpre.at[0]),
        pltpu.make_async_copy(dpre1, dpre_in.at[half:], sem_dpre.at[1]),
    ]
    loads, stores = [], []
    for k in range(width // PART):
        at = slice(k * PART, (k + 1) * PART)
        loads.append((
            pltpu.make_async_copy(rows0.at[:, at], rows_in.at[:half, at], sem_in.at[0, k]),
            pltpu.make_async_copy(rows1.at[:, at], rows_in.at[half:, at], sem_in.at[1, k]),
        ))
        stores.append(pltpu.make_async_copy(out_buf.at[at], out.at[at], sem_out.at[k]))
    for group in (first, *loads):
        for copy in group:
            copy.start()
    for copy in first:
        copy.wait()
    for k in range(width // PART):
        at = slice(k * PART, (k + 1) * PART)
        for copy in loads[k]:
            copy.wait()
        out_buf[at] = jnp.dot(
            rows_in[:, at].T, dpre_in[...], preferred_element_type=f32
        ).astype(bf16)
        stores[k].start()
    for copy in stores:
        copy.wait()


def encode_grad(rows, error):
    half, width = rows[0].shape
    mine = (error[0].shape[1] - width) // 2
    steps = width // PART
    return pl.pallas_call(
        encode_grad_kernel,
        out_shape=jax.ShapeDtypeStruct((width, mine), bf16),
        in_specs=[HBM] * 4,
        out_specs=HBM,
        scratch_shapes=[
            pltpu.VMEM((2 * half, width), bf16),
            pltpu.VMEM((2 * half, mine), bf16),
            pltpu.VMEM((width, mine), bf16),
            pltpu.SemaphoreType.DMA((2,)),
            pltpu.SemaphoreType.DMA((2, steps)),
            pltpu.SemaphoreType.DMA((steps,)),
        ],
        compiler_params=pltpu.CompilerParams(vmem_limit_bytes=GRAD_BYTES),
        cost_estimate=pl.CostEstimate(
            flops=4 * half * width * mine, bytes_accessed=7_000_000, transcendentals=0
        ),
        name="encode_grad",
    )(*rows, *error)


def per_device(resid_rows, w_encode, b_encode, w_decode, b_decode):
    local_rows, width = resid_rows.shape
    total_rows = local_rows * 16
    half = total_rows // 2
    rows = half // NWIDE
    factor = 1.0 / math.sqrt(total_rows)

    piece = rows // NZH
    at = (lax.axis_index("c") * 2 + lax.axis_index("zl")) * 4 + lax.axis_index("x")
    block = lax.dynamic_slice_in_dim(resid_rows, at * piece, piece, 0)
    pieces = spread(block, ZH, NZH)
    dec_float = w_decode.astype(f32)
    norms = jnp.sqrt(jnp.sum(dec_float * dec_float, axis=1) + 1e-06)
    slope0 = (0.5 * factor * norms).reshape(1, -1)
    bias0 = b_encode.reshape(1, -1)
    center = b_decode.reshape(1, -1)
    pieces, center, norms, slope0, slope1, bias0, bias1, enc1, dec1 = tie(
        pieces, center, norms.reshape(1, -1), slope0, swap(slope0), bias0, swap(bias0),
        swap(w_encode), swap(w_decode),
    )
    wide_shape = jax.ShapeDtypeStruct((NWIDE, rows, width), bf16)
    block, centered, enc1, dec1 = collect(pieces, center, enc1, dec1, NWIDE)
    centered = lax.all_to_all(centered, WIDE, 0, 0, tiled=True).reshape(half, width)

    active0, active1, codes0, codes1, part, centered = forward(
        centered, (w_encode, enc1), (w_decode, dec1), (bias0, bias1)
    )
    part = part.reshape(NWIDE, rows, width)
    part = lax.all_to_all(part, WIDE, 0, 0, tiled=True)
    part = small_kernel(
        reduce_kernel, jax.ShapeDtypeStruct((NZH, rows, width), bf16), part, name="reduce"
    )
    part = lax.all_to_all(part, ZH, 0, 0, tiled=True)
    error, block_sum = small_kernel(
        functools.partial(error_kernel, factor),
        (wide_shape, jax.ShapeDtypeStruct((width // 128, 128), f32)),
        part, block, name="error",
    )
    error = lax.all_to_all(error, WIDE, 0, 0, tiled=True).reshape(half, width)
    sums0, sums1, through, error = backward(
        error, (w_decode, dec1), (w_encode, enc1), (active0, active1), (slope0, slope1),
        block_sum, factor,
    )
    through = through + swap(through)
    through, centered, error, codes1, sums1 = tie(through, centered, error, codes1, sums1)
    their_codes = swap(codes1)
    their_error, their_rows = swap(error), swap(centered)
    through = spread(through, Z, NZ)
    grad_decode = decode_grad(
        (codes0, their_codes), (error, their_error), w_decode, norms, factor
    )
    through, grad_decode, their_rows = tie(through, grad_decode, their_rows)
    through = jnp.sum(spread(jnp.sum(through, axis=0), XY, NXY), axis=0).reshape(width)
    grad_encode = encode_grad((centered, their_rows), (error, their_error))
    grad_b_encode = (sums0 + swap(sums1)).reshape(-1)
    return (grad_encode, grad_b_encode, grad_decode, -through)


def solution(mesh):
    fine = Mesh(mesh.devices.reshape(2, 4, 2, 4, 4), ("zl", "x", "c", "zh", "y"))
    latents = LMAJ + LMIN
    in_specs = (P(LMIN, None), P(None, latents), P(latents), P(latents, None), P())
    out_specs = (P(None, latents), P(latents), P(latents, None), P())
    return jax.shard_map(
        per_device, mesh=fine, in_specs=in_specs, out_specs=out_specs, check_vma=False
    )
```

```python
import functools
import math

import jax
import jax.numpy as jnp
from jax import lax
from jax.experimental import pallas as pl
from jax.experimental.pallas import tpu as pltpu
from jax.sharding import Mesh, PartitionSpec as P

LMAJ = ("zl", "x", "c")
LMIN = ("zh", "y")
WIDE, NWIDE = ("zl", "x", "y"), 32
XY, NXY = ("x", "y"), 16
Z, NZ = ("zl", "zh"), 8
ZH, NZH = ("zh",), 4
f32, bf16 = jnp.float32, jnp.bfloat16
VMEM = pl.BlockSpec(memory_space=pltpu.VMEM)
HBM = pl.BlockSpec(memory_space=pl.ANY)
VMEM_BYTES = 16 * 1024 * 1024
SMALL_BYTES = 6 * 1024 * 1024
GRAD_BYTES = 24 * 1024 * 1024
PART = 896
ENC_PIECE = 448
DEC_PIECE = 48
NT = (((1,), (1,)), ((), ()))


def spread(block, axes, n):
    return lax.all_to_all(
        jnp.broadcast_to(block[None], (n,) + block.shape), axes, 0, 0, tiled=True
    )


def swap(block):
    return lax.ppermute(block, "c", [(0, 1), (1, 0)])


def tie(*values):
    return lax.optimization_barrier(values)


def small_kernel(body, out_shape, *args, name):
    return pl.pallas_call(
        body,
        out_shape=out_shape,
        in_specs=[VMEM] * len(args),
        out_specs=jax.tree.map(lambda _: VMEM, out_shape),
        compiler_params=pltpu.CompilerParams(vmem_limit_bytes=SMALL_BYTES),
        name=name,
    )(*args)


def repeat_into(out, value):
    for k in range(out.shape[0]):
        out[k] = value


def collect_kernel(pieces, bias, enc_hbm, dec_hbm, block, out, enc, dec, sem):
    first = lax.axis_index("c") == 0

    def load(source, to, rows, k):
        at = pl.ds(pl.multiple_of(k * rows, rows), rows)
        copy = pltpu.make_async_copy(source.at[at], to.at[at], sem.at[0])
        copy.start()
        copy.wait()

    @pl.when(first)
    def _():
        pl.loop(0, enc.shape[0] // ENC_PIECE)(functools.partial(load, enc_hbm, enc, ENC_PIECE))
        pl.loop(0, dec.shape[0] // DEC_PIECE)(functools.partial(load, dec_hbm, dec, DEC_PIECE))

    @pl.when(jnp.logical_not(first))
    def _():
        copies = (
            pltpu.make_async_copy(enc_hbm, enc, sem.at[0]),
            pltpu.make_async_copy(dec_hbm, dec, sem.at[1]),
        )
        for copy in copies:
            copy.start()
        for copy in copies:
            copy.wait()

    value = jnp.concatenate([pieces[k] for k in range(pieces.shape[0])], axis=0)
    value = (value.astype(f32) - bias[...]).astype(bf16)
    block[...] = value
    repeat_into(out, value)


def collect(pieces, bias, enc, dec, wide):
    count, rows, width = pieces.shape
    return pl.pallas_call(
        collect_kernel,
        out_shape=(
            jax.ShapeDtypeStruct((count * rows, width), bf16),
            jax.ShapeDtypeStruct((wide, count * rows, width), bf16),
            jax.ShapeDtypeStruct(enc.shape, bf16),
            jax.ShapeDtypeStruct(dec.shape, bf16),
        ),
        in_specs=[VMEM, VMEM, HBM, HBM],
        out_specs=(VMEM,) * 4,
        scratch_shapes=[pltpu.SemaphoreType.DMA((2,))],
        compiler_params=pltpu.CompilerParams(vmem_limit_bytes=SMALL_BYTES),
        name="collect",
    )(pieces, bias, enc, dec)


def reduce_kernel(parts, out):
    total = parts[0].astype(f32)
    for k in range(1, parts.shape[0]):
        total += parts[k].astype(f32)
    repeat_into(out, total.astype(bf16))


def error_kernel(factor, parts, block, out, block_sum):
    total = parts[0].astype(f32)
    for k in range(1, parts.shape[0]):
        total += parts[k].astype(f32)
    error = (total - block[...].astype(f32)).astype(bf16)
    repeat_into(out, error)
    row = (2.0 * factor / parts.shape[0]) * jnp.sum(error.astype(f32), axis=0, keepdims=True)
    for k in range(block_sum.shape[0]):
        block_sum[k : k + 1, :] = row[:, 128 * k : 128 * (k + 1)]


def add_kernel(mine, theirs, out):
    repeat_into(out, mine[...] + theirs[...])


def minus_sum_kernel(parts, out):
    total = parts[0]
    for k in range(1, parts.shape[0]):
        total += parts[k]
    repeat_into(out, -total)


def forward_kernel(
    rows, enc0, enc1, dec0, dec1, bias0, bias1,
    active0, active1, codes0_out, codes1_out, part, rows_out, codes0, codes1, sem,
):
    copies = [
        pltpu.make_async_copy(codes0, codes0_out, sem.at[0]),
        pltpu.make_async_copy(codes1, codes1_out, sem.at[1]),
        pltpu.make_async_copy(rows, rows_out, sem.at[2]),
    ]
    copies[2].start()
    for k, (enc, bias, active, codes) in enumerate((
        (enc0, bias0, active0, codes0),
        (enc1, bias1, active1, codes1),
    )):
        pre = jnp.dot(rows[...], enc[...], preferred_element_type=f32) + bias[...]
        value = jnp.maximum(pre, 0.0)
        active[...] = value
        codes[...] = (value * value).astype(bf16)
        copies[k].start()
    total = jnp.dot(codes0[...], dec0[...], preferred_element_type=f32)
    total += jnp.dot(codes1[...], dec1[...], preferred_element_type=f32)
    part[...] = total.astype(bf16)
    for copy in copies:
        copy.wait()


def forward(rows, enc, dec, bias):
    count, width = rows.shape
    mine = enc[0].shape[1]
    flat = jax.ShapeDtypeStruct((count, mine), f32)
    half = jax.ShapeDtypeStruct((count, mine), bf16)
    full = jax.ShapeDtypeStruct((count, width), bf16)
    return pl.pallas_call(
        forward_kernel,
        out_shape=(flat, flat, half, half, full, full),
        in_specs=[VMEM] * 7,
        out_specs=(VMEM, VMEM, HBM, HBM, VMEM, HBM),
        scratch_shapes=[
            pltpu.VMEM((count, mine), bf16),
            pltpu.VMEM((count, mine), bf16),
            pltpu.SemaphoreType.DMA((3,)),
        ],
        compiler_params=pltpu.CompilerParams(vmem_limit_bytes=VMEM_BYTES),
        cost_estimate=pl.CostEstimate(
            flops=8 * count * width * mine, bytes_accessed=16_000_000, transcendentals=0
        ),
        name="forward",
    )(rows, *enc, *dec, *bias)


def backward_kernel(
    factor, error, dec0, dec1, enc0, enc1, active0, active1, slope0, slope1, block_sum,
    sums0, sums1, through, out, rounded, sem,
):
    width, mine = error.shape[1], rounded.shape[2]
    copies = [
        pltpu.make_async_copy(rounded.at[0], out.at[:, width : width + mine], sem.at[0]),
        pltpu.make_async_copy(rounded.at[1], out.at[:, width + mine :], sem.at[1]),
        pltpu.make_async_copy(error, out.at[:, :width], sem.at[2]),
    ]
    copies[2].start()
    product = None
    for k, (dec, enc, active, slope, sums) in enumerate((
        (dec0, enc0, active0, slope0, sums0),
        (dec1, enc1, active1, slope1, sums1),
    )):
        back = lax.dot_general(error[...], dec[...], NT, preferred_element_type=f32)
        value = (2.0 * factor * back + slope[...]) * 2.0 * active[...]
        rounded[k] = value.astype(bf16)
        copies[k].start()
        total = jnp.sum(value, axis=0, keepdims=True)
        sums[...] = total
        first = total.astype(bf16)
        rest = total - first.astype(f32)
        second = rest.astype(bf16)
        third = (rest - second.astype(f32)).astype(bf16)
        parts = jnp.concatenate(
            [first, second, third, jnp.zeros((13, total.shape[1]), bf16)], axis=0
        )
        term = lax.dot_general(parts, enc[...], NT, preferred_element_type=f32)
        product = term if product is None else product + term
    row = product[0:1] + product[1:2] + product[2:3]
    for k in range(through.shape[0]):
        through[k : k + 1, :] = row[:, 128 * k : 128 * (k + 1)] - block_sum[k : k + 1, :]
    for copy in copies:
        copy.wait()


def backward(error, dec, enc, active, slope, block_sum, factor):
    count, width = error.shape
    mine = enc[0].shape[1]
    line = jax.ShapeDtypeStruct((1, mine), f32)
    return pl.pallas_call(
        functools.partial(backward_kernel, factor),
        out_shape=(
            line, line, jax.ShapeDtypeStruct(block_sum.shape, f32),
            jax.ShapeDtypeStruct((count, width + 2 * mine), bf16),
        ),
        in_specs=[VMEM] * 10,
        out_specs=(VMEM,) * 3 + (HBM,),
        scratch_shapes=[pltpu.VMEM((2, count, mine), bf16), pltpu.SemaphoreType.DMA((3,))],
        compiler_params=pltpu.CompilerParams(vmem_limit_bytes=VMEM_BYTES),
        cost_estimate=pl.CostEstimate(
            flops=6 * count * width * mine, bytes_accessed=15_000_000, transcendentals=0
        ),
        name="backward",
    )(error, *dec, *enc, *active, *slope, block_sum)


def decode_grad_kernel(
    factor, codes0, codes1, error0, error1, dec, norms, out,
    codes_in, error_in, dec_in, out_buf, sem_codes, sem_in, sem_out,
):
    half, width = error0.shape[0], dec.shape[1]
    first = [
        pltpu.make_async_copy(codes0, codes_in.at[:half], sem_codes.at[0]),
        pltpu.make_async_copy(codes1, codes_in.at[half:], sem_codes.at[1]),
    ]
    loads, stores = [], []
    for k in range(width // PART):
        at = slice(k * PART, (k + 1) * PART)
        loads.append((
            pltpu.make_async_copy(error0.at[:, at], error_in.at[:half, at], sem_in.at[0, k]),
            pltpu.make_async_copy(error1.at[:, at], error_in.at[half:, at], sem_in.at[1, k]),
            pltpu.make_async_copy(dec.at[:, at], dec_in.at[:, at], sem_in.at[2, k]),
        ))
        stores.append(pltpu.make_async_copy(out_buf.at[:, at], out.at[:, at], sem_out.at[k]))
    for group in (first, *loads):
        for copy in group:
            copy.start()
    for copy in first:
        copy.wait()
    codes = codes_in[...].T
    norm = jnp.broadcast_to(norms[...], (8, norms.shape[1])).T[:, :1]
    scale = 0.5 * factor * (jnp.sum(codes.astype(f32), axis=1, keepdims=True) / norm)
    for k in range(width // PART):
        at = slice(k * PART, (k + 1) * PART)
        for copy in loads[k]:
            copy.wait()
        grad = 2.0 * factor * jnp.dot(codes, error_in[:, at], preferred_element_type=f32)
        out_buf[:, at] = (grad + scale * dec_in[:, at].astype(f32)).astype(bf16)
        stores[k].start()
    for copy in stores:
        copy.wait()


def decode_grad(codes, error, dec, norms, factor):
    half = error[0].shape[0]
    mine, width = dec.shape
    steps = width // PART
    return pl.pallas_call(
        functools.partial(decode_grad_kernel, factor),
        out_shape=jax.ShapeDtypeStruct((mine, width), bf16),
        in_specs=[HBM] * 5 + [VMEM],
        out_specs=HBM,
        scratch_shapes=[
            pltpu.VMEM((2 * half, mine), bf16),
            pltpu.VMEM((2 * half, width), bf16),
            pltpu.VMEM((mine, width), bf16),
            pltpu.VMEM((mine, width), bf16),
            pltpu.SemaphoreType.DMA((2,)),
            pltpu.SemaphoreType.DMA((3, steps)),
            pltpu.SemaphoreType.DMA((steps,)),
        ],
        compiler_params=pltpu.CompilerParams(vmem_limit_bytes=GRAD_BYTES),
        cost_estimate=pl.CostEstimate(
            flops=4 * half * width * mine, bytes_accessed=10_000_000, transcendentals=0
        ),
        name="decode_grad",
    )(*codes, *error, dec, norms)


def encode_grad_kernel(
    rows0, rows1, error0, error1, out, rows_in, dpre_in, out_buf, sem_dpre, sem_in, sem_out
):
    half, width = rows0.shape
    mine = out.shape[1]
    dpre0 = error0.at[:, width : width + mine]
    dpre1 = error1.at[:, width + mine :]
    first = [
        pltpu.make_async_copy(dpre0, dpre_in.at[:half], sem_dpre.at[0]),
        pltpu.make_async_copy(dpre1, dpre_in.at[half:], sem_dpre.at[1]),
    ]
    loads, stores = [], []
    for k in range(width // PART):
        at = slice(k * PART, (k + 1) * PART)
        loads.append((
            pltpu.make_async_copy(rows0.at[:, at], rows_in.at[:half, at], sem_in.at[0, k]),
            pltpu.make_async_copy(rows1.at[:, at], rows_in.at[half:, at], sem_in.at[1, k]),
        ))
        stores.append(pltpu.make_async_copy(out_buf.at[at], out.at[at], sem_out.at[k]))
    for group in (first, *loads):
        for copy in group:
            copy.start()
    for copy in first:
        copy.wait()
    for k in range(width // PART):
        at = slice(k * PART, (k + 1) * PART)
        for copy in loads[k]:
            copy.wait()
        out_buf[at] = jnp.dot(
            rows_in[:, at].T, dpre_in[...], preferred_element_type=f32
        ).astype(bf16)
        stores[k].start()
    for copy in stores:
        copy.wait()


def encode_grad(rows, error):
    half, width = rows[0].shape
    mine = (error[0].shape[1] - width) // 2
    steps = width // PART
    return pl.pallas_call(
        encode_grad_kernel,
        out_shape=jax.ShapeDtypeStruct((width, mine), bf16),
        in_specs=[HBM] * 4,
        out_specs=HBM,
        scratch_shapes=[
            pltpu.VMEM((2 * half, width), bf16),
            pltpu.VMEM((2 * half, mine), bf16),
            pltpu.VMEM((width, mine), bf16),
            pltpu.SemaphoreType.DMA((2,)),
            pltpu.SemaphoreType.DMA((2, steps)),
            pltpu.SemaphoreType.DMA((steps,)),
        ],
        compiler_params=pltpu.CompilerParams(vmem_limit_bytes=GRAD_BYTES),
        cost_estimate=pl.CostEstimate(
            flops=4 * half * width * mine, bytes_accessed=7_000_000, transcendentals=0
        ),
        name="encode_grad",
    )(*rows, *error)


def per_device(resid_rows, w_encode, b_encode, w_decode, b_decode):
    local_rows, width = resid_rows.shape
    total_rows = local_rows * 16
    half = total_rows // 2
    rows = half // NWIDE
    factor = 1.0 / math.sqrt(total_rows)

    piece = rows // NZH
    at = (lax.axis_index("c") * 2 + lax.axis_index("zl")) * 4 + lax.axis_index("x")
    block = lax.dynamic_slice_in_dim(resid_rows, at * piece, piece, 0)
    pieces = spread(block, ZH, NZH)
    dec_float = w_decode.astype(f32)
    norms = jnp.sqrt(jnp.sum(dec_float * dec_float, axis=1) + 1e-06)
    slope0 = (0.5 * factor * norms).reshape(1, -1)
    bias0 = b_encode.reshape(1, -1)
    center = b_decode.reshape(1, -1)
    pieces, center, norms, slope0, slope1, bias0, bias1, enc1, dec1 = tie(
        pieces, center, norms.reshape(1, -1), slope0, swap(slope0), bias0, swap(bias0),
        swap(w_encode), swap(w_decode),
    )
    wide_shape = jax.ShapeDtypeStruct((NWIDE, rows, width), bf16)
    block, centered, enc1, dec1 = collect(pieces, center, enc1, dec1, NWIDE)
    centered = lax.all_to_all(centered, WIDE, 0, 0, tiled=True).reshape(half, width)

    active0, active1, codes0, codes1, part, centered = forward(
        centered, (w_encode, enc1), (w_decode, dec1), (bias0, bias1)
    )
    part = part.reshape(NWIDE, rows, width)
    part = lax.all_to_all(part, WIDE, 0, 0, tiled=True)
    part = small_kernel(
        reduce_kernel, jax.ShapeDtypeStruct((NZH, rows, width), bf16), part, name="reduce"
    )
    part = lax.all_to_all(part, ZH, 0, 0, tiled=True)
    error, block_sum = small_kernel(
        functools.partial(error_kernel, factor),
        (wide_shape, jax.ShapeDtypeStruct((width // 128, 128), f32)),
        part, block, name="error",
    )
    error = lax.all_to_all(error, WIDE, 0, 0, tiled=True).reshape(half, width)
    sums0, sums1, through, error = backward(
        error, (w_decode, dec1), (w_encode, enc1), (active0, active1), (slope0, slope1),
        block_sum, factor,
    )
    lines = through.shape
    through = small_kernel(
        add_kernel, jax.ShapeDtypeStruct((NZ,) + lines, f32), through, swap(through), name="add"
    )
    through, centered, error, codes1, sums1 = tie(through, centered, error, codes1, sums1)
    their_codes = swap(codes1)
    their_error, their_rows = swap(error), swap(centered)
    through = lax.all_to_all(through, Z, 0, 0, tiled=True)
    grad_b_encode = (sums0 + swap(sums1)).reshape(-1)
    grad_decode = decode_grad(
        (codes0, their_codes), (error, their_error), w_decode, norms, factor
    )
    through, grad_decode, their_rows, grad_b_encode = tie(
        through, grad_decode, their_rows, grad_b_encode
    )
    through = small_kernel(
        minus_sum_kernel, jax.ShapeDtypeStruct((NXY,) + lines, f32), through, name="minus_sum"
    )
    grad_b_decode = jnp.sum(lax.all_to_all(through, XY, 0, 0, tiled=True), axis=0)
    grad_encode = encode_grad((centered, their_rows), (error, their_error))
    return (grad_encode, grad_b_encode, grad_decode, grad_b_decode.reshape(width))


def solution(mesh):
    fine = Mesh(mesh.devices.reshape(2, 4, 2, 4, 4), ("zl", "x", "c", "zh", "y"))
    latents = LMAJ + LMIN
    in_specs = (P(LMIN, None), P(None, latents), P(latents), P(latents, None), P())
    out_specs = (P(None, latents), P(latents), P(latents, None), P())
    return jax.shard_map(
        per_device, mesh=fine, in_specs=in_specs, out_specs=out_specs, check_vma=False
    )
```

```python
import functools
import math

import jax
import jax.numpy as jnp
from jax import lax
from jax.experimental import pallas as pl
from jax.experimental.pallas import tpu as pltpu
from jax.sharding import Mesh, PartitionSpec as P

LMAJ = ("zl", "x", "c")
LMIN = ("zh", "y")
WIDE, NWIDE = ("zl", "x", "y"), 32
XY, NXY = ("x", "y"), 16
ZC, NZC = ("zl", "c", "zh"), 16
ZH, NZH = ("zh",), 4
f32, bf16 = jnp.float32, jnp.bfloat16
VMEM = pl.BlockSpec(memory_space=pltpu.VMEM)
HBM = pl.BlockSpec(memory_space=pl.ANY)
VMEM_BYTES = 16 * 1024 * 1024
SMALL_BYTES = 6 * 1024 * 1024
GRAD_BYTES = 24 * 1024 * 1024
PART = 896
ENC_PIECE = 448
DEC_PIECE = 48
NT = (((1,), (1,)), ((), ()))


def spread(block, axes, n):
    return lax.all_to_all(
        jnp.broadcast_to(block[None], (n,) + block.shape), axes, 0, 0, tiled=True
    )


def swap(block):
    return lax.ppermute(block, "c", [(0, 1), (1, 0)])


def tie(*values):
    return lax.optimization_barrier(values)


def small_kernel(body, out_shape, *args, name):
    return pl.pallas_call(
        body,
        out_shape=out_shape,
        in_specs=[VMEM] * len(args),
        out_specs=jax.tree.map(lambda _: VMEM, out_shape),
        compiler_params=pltpu.CompilerParams(vmem_limit_bytes=SMALL_BYTES),
        name=name,
    )(*args)


def repeat_into(out, value):
    for k in range(out.shape[0]):
        out[k] = value


def collect_kernel(pieces, bias, enc_hbm, dec_hbm, block, out, enc, dec, sem):
    first = lax.axis_index("c") == 0

    def load(source, to, rows, k):
        at = pl.ds(pl.multiple_of(k * rows, rows), rows)
        copy = pltpu.make_async_copy(source.at[at], to.at[at], sem.at[0])
        copy.start()
        copy.wait()

    @pl.when(first)
    def _():
        pl.loop(0, enc.shape[0] // ENC_PIECE)(functools.partial(load, enc_hbm, enc, ENC_PIECE))
        pl.loop(0, dec.shape[0] // DEC_PIECE)(functools.partial(load, dec_hbm, dec, DEC_PIECE))

    @pl.when(jnp.logical_not(first))
    def _():
        copies = (
            pltpu.make_async_copy(enc_hbm, enc, sem.at[0]),
            pltpu.make_async_copy(dec_hbm, dec, sem.at[1]),
        )
        for copy in copies:
            copy.start()
        for copy in copies:
            copy.wait()

    value = jnp.concatenate([pieces[k] for k in range(pieces.shape[0])], axis=0)
    value = (value.astype(f32) - bias[...]).astype(bf16)
    block[...] = value
    repeat_into(out, value)


def collect(pieces, bias, enc, dec, wide):
    count, rows, width = pieces.shape
    return pl.pallas_call(
        collect_kernel,
        out_shape=(
            jax.ShapeDtypeStruct((count * rows, width), bf16),
            jax.ShapeDtypeStruct((wide, count * rows, width), bf16),
            jax.ShapeDtypeStruct(enc.shape, bf16),
            jax.ShapeDtypeStruct(dec.shape, bf16),
        ),
        in_specs=[VMEM, VMEM, HBM, HBM],
        out_specs=(VMEM,) * 4,
        scratch_shapes=[pltpu.SemaphoreType.DMA((2,))],
        compiler_params=pltpu.CompilerParams(vmem_limit_bytes=SMALL_BYTES),
        name="collect",
    )(pieces, bias, enc, dec)


def reduce_kernel(parts, out):
    total = parts[0].astype(f32)
    for k in range(1, parts.shape[0]):
        total += parts[k].astype(f32)
    repeat_into(out, total.astype(bf16))


def error_kernel(factor, parts, block, out, block_sum):
    total = parts[0].astype(f32)
    for k in range(1, parts.shape[0]):
        total += parts[k].astype(f32)
    error = (total - block[...].astype(f32)).astype(bf16)
    repeat_into(out, error)
    row = (2.0 * factor / parts.shape[0]) * jnp.sum(error.astype(f32), axis=0, keepdims=True)
    for k in range(block_sum.shape[0]):
        block_sum[k : k + 1, :] = row[:, 128 * k : 128 * (k + 1)]


def minus_sum_kernel(parts, out):
    total = parts[0]
    for k in range(1, parts.shape[0]):
        total += parts[k]
    repeat_into(out, -total)


def forward_kernel(
    rows, enc0, enc1, dec0, dec1, bias0, bias1,
    active0, active1, codes0_out, codes1_out, part, rows_out, codes0, codes1, sem,
):
    copies = [
        pltpu.make_async_copy(codes0, codes0_out, sem.at[0]),
        pltpu.make_async_copy(codes1, codes1_out, sem.at[1]),
        pltpu.make_async_copy(rows, rows_out, sem.at[2]),
    ]
    copies[2].start()
    for k, (enc, bias, active, codes) in enumerate((
        (enc0, bias0, active0, codes0),
        (enc1, bias1, active1, codes1),
    )):
        pre = jnp.dot(rows[...], enc[...], preferred_element_type=f32) + bias[...]
        value = jnp.maximum(pre, 0.0)
        active[...] = value
        codes[...] = (value * value).astype(bf16)
        copies[k].start()
    total = jnp.dot(codes0[...], dec0[...], preferred_element_type=f32)
    total += jnp.dot(codes1[...], dec1[...], preferred_element_type=f32)
    part[...] = total.astype(bf16)
    for copy in copies:
        copy.wait()


def forward(rows, enc, dec, bias):
    count, width = rows.shape
    mine = enc[0].shape[1]
    flat = jax.ShapeDtypeStruct((count, mine), f32)
    half = jax.ShapeDtypeStruct((count, mine), bf16)
    full = jax.ShapeDtypeStruct((count, width), bf16)
    return pl.pallas_call(
        forward_kernel,
        out_shape=(flat, flat, half, half, full, full),
        in_specs=[VMEM] * 7,
        out_specs=(VMEM, VMEM, HBM, HBM, VMEM, HBM),
        scratch_shapes=[
            pltpu.VMEM((count, mine), bf16),
            pltpu.VMEM((count, mine), bf16),
            pltpu.SemaphoreType.DMA((3,)),
        ],
        compiler_params=pltpu.CompilerParams(vmem_limit_bytes=VMEM_BYTES),
        cost_estimate=pl.CostEstimate(
            flops=8 * count * width * mine, bytes_accessed=16_000_000, transcendentals=0
        ),
        name="forward",
    )(rows, *enc, *dec, *bias)


def backward_kernel(
    factor, error, dec0, dec1, enc0, enc1, active0, active1, slope0, slope1, block_sum,
    sums0, sums1, through, out, rounded, sem,
):
    width, mine = error.shape[1], rounded.shape[2]
    copies = [
        pltpu.make_async_copy(rounded.at[0], out.at[:, width : width + mine], sem.at[0]),
        pltpu.make_async_copy(rounded.at[1], out.at[:, width + mine :], sem.at[1]),
        pltpu.make_async_copy(error, out.at[:, :width], sem.at[2]),
    ]
    copies[2].start()
    product = None
    for k, (dec, enc, active, slope, sums) in enumerate((
        (dec0, enc0, active0, slope0, sums0),
        (dec1, enc1, active1, slope1, sums1),
    )):
        back = lax.dot_general(error[...], dec[...], NT, preferred_element_type=f32)
        value = (2.0 * factor * back + slope[...]) * 2.0 * active[...]
        rounded[k] = value.astype(bf16)
        copies[k].start()
        total = jnp.sum(value, axis=0, keepdims=True)
        sums[...] = total
        first = total.astype(bf16)
        rest = total - first.astype(f32)
        second = rest.astype(bf16)
        third = (rest - second.astype(f32)).astype(bf16)
        parts = jnp.concatenate(
            [first, second, third, jnp.zeros((13, total.shape[1]), bf16)], axis=0
        )
        term = lax.dot_general(parts, enc[...], NT, preferred_element_type=f32)
        product = term if product is None else product + term
    row = product[0:1] + product[1:2] + product[2:3]
    lines = [row[:, 128 * k : 128 * (k + 1)] for k in range(through.shape[1])]
    repeat_into(through, jnp.concatenate(lines, axis=0) - block_sum[...])
    for copy in copies:
        copy.wait()


def backward(error, dec, enc, active, slope, block_sum, factor):
    count, width = error.shape
    mine = enc[0].shape[1]
    line = jax.ShapeDtypeStruct((1, mine), f32)
    return pl.pallas_call(
        functools.partial(backward_kernel, factor),
        out_shape=(
            line, line, jax.ShapeDtypeStruct((NZC,) + block_sum.shape, f32),
            jax.ShapeDtypeStruct((count, width + 2 * mine), bf16),
        ),
        in_specs=[VMEM] * 10,
        out_specs=(VMEM,) * 3 + (HBM,),
        scratch_shapes=[pltpu.VMEM((2, count, mine), bf16), pltpu.SemaphoreType.DMA((3,))],
        compiler_params=pltpu.CompilerParams(vmem_limit_bytes=VMEM_BYTES),
        cost_estimate=pl.CostEstimate(
            flops=6 * count * width * mine, bytes_accessed=15_000_000, transcendentals=0
        ),
        name="backward",
    )(error, *dec, *enc, *active, *slope, block_sum)


def decode_grad_kernel(
    factor, codes0, codes1, error0, error1, dec, norms, out,
    codes_in, error_in, dec_in, out_buf, sem_codes, sem_in, sem_out,
):
    half, width = error0.shape[0], dec.shape[1]
    first = [
        pltpu.make_async_copy(codes0, codes_in.at[:half], sem_codes.at[0]),
        pltpu.make_async_copy(codes1, codes_in.at[half:], sem_codes.at[1]),
    ]
    loads, stores = [], []
    for k in range(width // PART):
        at = slice(k * PART, (k + 1) * PART)
        loads.append((
            pltpu.make_async_copy(error0.at[:, at], error_in.at[:half, at], sem_in.at[0, k]),
            pltpu.make_async_copy(error1.at[:, at], error_in.at[half:, at], sem_in.at[1, k]),
            pltpu.make_async_copy(dec.at[:, at], dec_in.at[:, at], sem_in.at[2, k]),
        ))
        stores.append(pltpu.make_async_copy(out_buf.at[:, at], out.at[:, at], sem_out.at[k]))
    for group in (first, *loads):
        for copy in group:
            copy.start()
    for copy in first:
        copy.wait()
    codes = codes_in[...].T
    norm = jnp.broadcast_to(norms[...], (8, norms.shape[1])).T[:, :1]
    scale = 0.5 * factor * (jnp.sum(codes.astype(f32), axis=1, keepdims=True) / norm)
    for k in range(width // PART):
        at = slice(k * PART, (k + 1) * PART)
        for copy in loads[k]:
            copy.wait()
        grad = 2.0 * factor * jnp.dot(codes, error_in[:, at], preferred_element_type=f32)
        out_buf[:, at] = (grad + scale * dec_in[:, at].astype(f32)).astype(bf16)
        stores[k].start()
    for copy in stores:
        copy.wait()


def decode_grad(codes, error, dec, norms, factor):
    half = error[0].shape[0]
    mine, width = dec.shape
    steps = width // PART
    return pl.pallas_call(
        functools.partial(decode_grad_kernel, factor),
        out_shape=jax.ShapeDtypeStruct((mine, width), bf16),
        in_specs=[HBM] * 5 + [VMEM],
        out_specs=HBM,
        scratch_shapes=[
            pltpu.VMEM((2 * half, mine), bf16),
            pltpu.VMEM((2 * half, width), bf16),
            pltpu.VMEM((mine, width), bf16),
            pltpu.VMEM((mine, width), bf16),
            pltpu.SemaphoreType.DMA((2,)),
            pltpu.SemaphoreType.DMA((3, steps)),
            pltpu.SemaphoreType.DMA((steps,)),
        ],
        compiler_params=pltpu.CompilerParams(vmem_limit_bytes=GRAD_BYTES),
        cost_estimate=pl.CostEstimate(
            flops=4 * half * width * mine, bytes_accessed=10_000_000, transcendentals=0
        ),
        name="decode_grad",
    )(*codes, *error, dec, norms)


def encode_grad_kernel(
    rows0, rows1, error0, error1, out, rows_in, dpre_in, out_buf, sem_dpre, sem_in, sem_out
):
    half, width = rows0.shape
    mine = out.shape[1]
    dpre0 = error0.at[:, width : width + mine]
    dpre1 = error1.at[:, width + mine :]
    first = [
        pltpu.make_async_copy(dpre0, dpre_in.at[:half], sem_dpre.at[0]),
        pltpu.make_async_copy(dpre1, dpre_in.at[half:], sem_dpre.at[1]),
    ]
    loads, stores = [], []
    for k in range(width // PART):
        at = slice(k * PART, (k + 1) * PART)
        loads.append((
            pltpu.make_async_copy(rows0.at[:, at], rows_in.at[:half, at], sem_in.at[0, k]),
            pltpu.make_async_copy(rows1.at[:, at], rows_in.at[half:, at], sem_in.at[1, k]),
        ))
        stores.append(pltpu.make_async_copy(out_buf.at[at], out.at[at], sem_out.at[k]))
    for group in (first, *loads):
        for copy in group:
            copy.start()
    for copy in first:
        copy.wait()
    for k in range(width // PART):
        at = slice(k * PART, (k + 1) * PART)
        for copy in loads[k]:
            copy.wait()
        out_buf[at] = jnp.dot(
            rows_in[:, at].T, dpre_in[...], preferred_element_type=f32
        ).astype(bf16)
        stores[k].start()
    for copy in stores:
        copy.wait()


def encode_grad(rows, error):
    half, width = rows[0].shape
    mine = (error[0].shape[1] - width) // 2
    steps = width // PART
    return pl.pallas_call(
        encode_grad_kernel,
        out_shape=jax.ShapeDtypeStruct((width, mine), bf16),
        in_specs=[HBM] * 4,
        out_specs=HBM,
        scratch_shapes=[
            pltpu.VMEM((2 * half, width), bf16),
            pltpu.VMEM((2 * half, mine), bf16),
            pltpu.VMEM((width, mine), bf16),
            pltpu.SemaphoreType.DMA((2,)),
            pltpu.SemaphoreType.DMA((2, steps)),
            pltpu.SemaphoreType.DMA((steps,)),
        ],
        compiler_params=pltpu.CompilerParams(vmem_limit_bytes=GRAD_BYTES),
        cost_estimate=pl.CostEstimate(
            flops=4 * half * width * mine, bytes_accessed=7_000_000, transcendentals=0
        ),
        name="encode_grad",
    )(*rows, *error)


def per_device(resid_rows, w_encode, b_encode, w_decode, b_decode):
    local_rows, width = resid_rows.shape
    total_rows = local_rows * 16
    half = total_rows // 2
    rows = half // NWIDE
    factor = 1.0 / math.sqrt(total_rows)

    piece = rows // NZH
    at = (lax.axis_index("c") * 2 + lax.axis_index("zl")) * 4 + lax.axis_index("x")
    block = lax.dynamic_slice_in_dim(resid_rows, at * piece, piece, 0)
    pieces = spread(block, ZH, NZH)
    dec_float = w_decode.astype(f32)
    norms = jnp.sqrt(jnp.sum(dec_float * dec_float, axis=1) + 1e-06)
    slope0 = (0.5 * factor * norms).reshape(1, -1)
    bias0 = b_encode.reshape(1, -1)
    center = b_decode.reshape(1, -1)
    pieces, center, norms, slope0, slope1, bias0, bias1, enc1, dec1 = tie(
        pieces, center, norms.reshape(1, -1), slope0, swap(slope0), bias0, swap(bias0),
        swap(w_encode), swap(w_decode),
    )
    wide_shape = jax.ShapeDtypeStruct((NWIDE, rows, width), bf16)
    block, centered, enc1, dec1 = collect(pieces, center, enc1, dec1, NWIDE)
    centered = lax.all_to_all(centered, WIDE, 0, 0, tiled=True).reshape(half, width)

    active0, active1, codes0, codes1, part, centered = forward(
        centered, (w_encode, enc1), (w_decode, dec1), (bias0, bias1)
    )
    part = part.reshape(NWIDE, rows, width)
    part = lax.all_to_all(part, WIDE, 0, 0, tiled=True)
    part = small_kernel(
        reduce_kernel, jax.ShapeDtypeStruct((NZH, rows, width), bf16), part, name="reduce"
    )
    part = lax.all_to_all(part, ZH, 0, 0, tiled=True)
    error, block_sum = small_kernel(
        functools.partial(error_kernel, factor),
        (wide_shape, jax.ShapeDtypeStruct((width // 128, 128), f32)),
        part, block, name="error",
    )
    error = lax.all_to_all(error, WIDE, 0, 0, tiled=True).reshape(half, width)
    sums0, sums1, through, error = backward(
        error, (w_decode, dec1), (w_encode, enc1), (active0, active1), (slope0, slope1),
        block_sum, factor,
    )
    through, centered, error, codes1, sums1 = tie(through, centered, error, codes1, sums1)
    their_codes = swap(codes1)
    their_error, their_rows = swap(error), swap(centered)
    through = lax.all_to_all(through, ZC, 0, 0, tiled=True)
    grad_b_encode = (sums0 + swap(sums1)).reshape(-1)
    grad_decode = decode_grad(
        (codes0, their_codes), (error, their_error), w_decode, norms, factor
    )
    through, grad_decode, their_rows, grad_b_encode = tie(
        through, grad_decode, their_rows, grad_b_encode
    )
    through = small_kernel(
        minus_sum_kernel, jax.ShapeDtypeStruct((NXY,) + block_sum.shape, f32), through, name="minus_sum"
    )
    grad_b_decode = jnp.sum(lax.all_to_all(through, XY, 0, 0, tiled=True), axis=0)
    grad_encode = encode_grad((centered, their_rows), (error, their_error))
    return (grad_encode, grad_b_encode, grad_decode, grad_b_decode.reshape(width))


def solution(mesh):
    fine = Mesh(mesh.devices.reshape(2, 4, 2, 4, 4), ("zl", "x", "c", "zh", "y"))
    latents = LMAJ + LMIN
    in_specs = (P(LMIN, None), P(None, latents), P(latents), P(latents, None), P())
    out_specs = (P(None, latents), P(latents), P(latents, None), P())
    return jax.shard_map(
        per_device, mesh=fine, in_specs=in_specs, out_specs=out_specs, check_vma=False
    )
```
